1024 devices in a mesh: expert: 64 (over x, y), dp: 16 (over z, core).
Axes of the slice: x: 8, y: 8, z: 8, core: 2. Of those that a mesh axis runs over, the one named last changes fastest.
Arguments:
- tokens: bfloat16 [131072, 2048], P(('expert', 'dp')), may hold values from -6 to 6
- cotangent: bfloat16 [131072, 2048], P(('expert', 'dp')), may hold values from -6 to 6
- expert_ids: int32 [131072, 1], P(('expert', 'dp')), may hold values from 0 to 63; in each aligned block of 128 rows (0 to 127, 128 to 255, ...) at most 3 rows name the same one
- route_weight: float32 [131072, 1], P(('expert', 'dp')), may hold values from 0.25 to 1
- w_gate: bfloat16 [64, 2048, 768], P('expert'), may hold values from -0.125 to 0.125
- w_up: bfloat16 [64, 2048, 768], P('expert'), may hold values from -0.125 to 0.125
- w_down: bfloat16 [2048, 64, 768], P('dp', 'expert'), may hold values from -0.21875 to 0.21875
Outputs:
- token_grad: bfloat16 [131072, 2048], P(('expert', 'dp'))
- down_grad: float32 [2048, 64, 768], P('dp', 'expert')
The draws below stay inside these ranges and needn't reach their ends.
Inputs may be any that keep to these rules, and one draw needn't show every extreme that they name: `expert_ids`: each token names 1 different experts. Among the 128 tokens of one device no expert is named more than 3 times, a bound that some block reaches.
All inputs are finite; a program needn't handle non-finite values.
Results may differ from the reference program's by a relative error of at most 0.02.
Values may be sent and summed in bfloat16 or wider, within the bound.
No kernel may reach another device: no remote copies, remote signals or barrier semaphores. Data moves between devices by JAX's collectives and lax.ppermute only.
A program may use at most 64 MiB of HBM per device.

```python
import math
import jax
import jax.numpy as jnp
import numpy as np
from jax import lax

D = 2048
FF = 768
TOPK = 1
TOK_DEV = 128
EXPERTS = 64
TOKENS = 131072
CAP = 3
N_EXPERT = 64
N_DP = 16


def spiked(result, rng, source, target, shards_of, factor):
    def block_of(axis_at):
        return (jnp.arange(result.shape[axis_at]) // (result.shape[axis_at] // shards_of)).reshape((-1,) + (1,) * (result.ndim - 1 - axis_at))

    first = jax.random.permutation(rng, shards_of)[block_of(target)]
    other_side = (block_of(target) + shards_of // 2) % shards_of
    return jnp.where((block_of(source) == first) | (block_of(source) == other_side), factor * result, result)


def shard_levels(stream_key, dims, cuts, smallest, high):
    factor_of, own = 1.0, jax.random.fold_in(stream_key, 6)
    for dim, blocks in cuts:
        steps = jnp.exp(jax.random.uniform(jax.random.fold_in(own, dim), (blocks,), jnp.float32, smallest / len(cuts), high / len(cuts)))
        factor_of = factor_of * jnp.repeat(steps, dims[dim] // blocks).reshape([-1 if axis == dim else 1 for axis in range(len(dims))])
    return factor_of


def routed_block(rng, own, number, rows, amount, top, reach, skew):
    ranking = jax.random.permutation(rng, amount)
    heavy_load, ordinary = portions_of(amount, rows * top, reach, skew, True), portions_of(amount, rows * top, reach, skew, False)
    places = jnp.arange(amount)

    def named(tallies, rotation):
        used = int((tallies > 0).sum())
        fixed = max(1, used // 4)
        passed = fixed + (places - fixed + rotation * (used - fixed)) % max(1, amount - fixed)
        return jnp.zeros((amount,), jnp.int32).at[ranking[jnp.where(places < fixed, places, passed)]].set(jnp.asarray(tallies, jnp.int32))

    tallies = jnp.where(number % 4 == 0, named(heavy_load, number // 4), named(ordinary, number - number // 4 - 1))
    mixed = jax.random.permutation(jax.random.fold_in(own, 3), amount)
    giver, sink = mixed[0:amount // 2 * 2:2], mixed[1:amount // 2 * 2:2]
    slack = jnp.minimum(tallies[giver] - 1, reach - tallies[sink]) // 2
    slack = jnp.where((giver == ranking[0]) | (sink == ranking[0]) | (tallies[sink] == 0), 0, jnp.maximum(slack, 0))
    passed = jax.random.randint(jax.random.fold_in(own, 4), (amount // 2,), 0, 1 << 20) % (slack + 1)
    tallies = tallies.at[giver].add(-passed).at[sink].add(passed)
    items = jnp.searchsorted(jnp.cumsum(tallies), jnp.arange(rows * top), side="right").astype(jnp.int32)
    table = items.reshape(top, rows).T
    table = table[jax.random.permutation(jax.random.fold_in(own, 1), rows)]
    rotation = jax.random.randint(jax.random.fold_in(own, 2), (rows, 1), 0, top)
    return jnp.take_along_axis(table, (jnp.arange(top)[None, :] + rotation) % top, axis=1)


def portions_of(amount, total, most, slope, full):
    weights = [(1 << 20) // math.isqrt(standing ** slope) + 1 for standing in range(1, amount + 1)]
    largest = most if full else min(most, max(-(-total // amount), total * weights[0] // sum(weights)))
    least = 1 if total - largest >= amount - 1 else 0
    holding, rest = [largest] + [least] * (amount - 1), total - largest - least * (amount - 1)
    while rest > 0:
        candidates = [i for i in range(1, amount) if holding[i] < largest] or [i for i in range(1, amount) if holding[i] < most]
        whole, budget = sum([weights[i] for i in candidates]), rest
        for i in candidates:
            addition = min(most - holding[i], max(1, budget * weights[i] // whole), rest)
            holding[i] = holding[i] + addition
            rest = rest - addition
    return np.array(holding)


def centred(own_key, dims, deviation, most, pieces=(), held_as=jnp.bfloat16):
    drawn = deviation * jax.random.normal(own_key, dims, jnp.float32)
    if pieces:
        drawn = drawn * shard_levels(own_key, dims, pieces, -0.22, 0.18)
    return jnp.clip(drawn, -most, most).astype(held_as)


def heavy_noise(stream_key, shape, scale, limit, pieces, heavy, kind=jnp.bfloat16):
    entries = scale * jax.random.normal(stream_key, shape, jnp.float32)
    if pieces:
        entries = entries * shard_levels(stream_key, shape, pieces, -0.22, 0.18)
    return jnp.clip(spiked(entries, jax.random.fold_in(stream_key, 3), *heavy), -limit, limit).astype(kind)


def setup_inputs(seed: int = 0) -> dict:
    arg_keys = jax.random.split(jax.random.key(seed), 8)
    tokens = centred(arg_keys[0], (TOKENS, D), 1.0, 6.0, ((0, 1024),))
    cotangent = heavy_noise(arg_keys[1], (TOKENS, D), 0.25, 6.0, ((0, 1024),), (0, 1, 1024, 6.0))
    expert_ids_keys = jax.random.split(jax.random.fold_in(arg_keys[2], 1), TOKENS // TOK_DEV)
    expert_ids_turns = jax.random.permutation(jax.random.fold_in(arg_keys[2], 3), TOKENS // TOK_DEV)
    expert_ids = jax.vmap(lambda own, number: routed_block(jax.random.fold_in(arg_keys[2], 2), own, number, TOK_DEV, EXPERTS, TOPK, CAP, 2))(expert_ids_keys, expert_ids_turns).reshape((TOKENS, TOPK))
    route_weight = jnp.clip(0.25 + 0.75 * jax.random.uniform(arg_keys[3], (TOKENS, TOPK), jnp.float32) ** shard_levels(arg_keys[3], (TOKENS, TOPK), ((0, 1024),), -0.2, 0.2), 0.25, 1.0)
    w_gate = centred(arg_keys[4], (EXPERTS, D, FF), D ** -0.5, 0.125, ((0, 64),))
    w_up = centred(arg_keys[5], (EXPERTS, D, FF), D ** -0.5, 0.125, ((0, 64),))
    w_down = centred(arg_keys[6], (D, EXPERTS, FF), FF ** -0.5, 0.21875, ((0, 16), (1, 64)))
    return dict(tokens=tokens, cotangent=cotangent, expert_ids=expert_ids, route_weight=route_weight, w_gate=w_gate, w_up=w_up, w_down=w_down)


def expert_pass(index, table_row, tokens_pad, cot_pad, weight_pad, w_gate, w_up, w_down):
    token_index = table_row // TOPK
    rows = tokens_pad[token_index]
    scaled = (weight_pad[table_row][:, None] * cot_pad[token_index].astype(jnp.float32)).astype(jnp.bfloat16)
    gate_weight = w_gate[index]
    up_weight = w_up[index]
    down_weight = w_down[:, index, :]
    gate = jnp.dot(rows, gate_weight, preferred_element_type=jnp.float32)
    up = jnp.dot(rows, up_weight, preferred_element_type=jnp.float32)
    hidden = (jax.nn.silu(gate) * up).astype(jnp.bfloat16)
    hidden_grad = jnp.dot(scaled, down_weight, preferred_element_type=jnp.float32)
    sig = jax.nn.sigmoid(gate)
    gate_grad = (hidden_grad * up * sig * (1.0 + gate * (1.0 - sig))).astype(jnp.bfloat16)
    up_grad = (hidden_grad * (gate * sig)).astype(jnp.bfloat16)
    token_part = (jnp.dot(gate_grad, gate_weight.T, preferred_element_type=jnp.float32)
                  + jnp.dot(up_grad, up_weight.T, preferred_element_type=jnp.float32)).astype(jnp.bfloat16)
    grouped_cot = scaled.reshape(N_EXPERT, N_DP, CAP, D).astype(jnp.float32)
    grouped_hidden = hidden.reshape(N_EXPERT, N_DP, CAP, FF).astype(jnp.float32)
    partial_value = jnp.einsum('ircd,ircf->rdf', grouped_cot, grouped_hidden, precision=lax.Precision.HIGHEST)
    rounded = lax.optimization_barrier(partial_value.astype(jnp.bfloat16)).astype(jnp.float32)
    return token_part, jnp.sum(rounded, axis=0)


def reference(tokens, cotangent, expert_ids, route_weight, w_gate, w_up, w_down):
    blocks = N_EXPERT * N_DP
    assigned = TOK_DEV * TOPK
    ids = expert_ids.reshape(blocks, assigned)
    choose = (ids[:, :, None] == jnp.arange(EXPERTS, dtype=jnp.int32)[None, None, :]).astype(jnp.int32)
    rank = jnp.sum((jnp.cumsum(choose, axis=1) - choose) * choose, axis=2).astype(jnp.int32)
    block_index = jnp.arange(blocks, dtype=jnp.int32)[:, None]
    position = ((ids * blocks + block_index) * CAP + rank).astype(jnp.int32)
    global_id = jnp.arange(blocks * assigned, dtype=jnp.int32).reshape(blocks, assigned)
    table = jnp.full((EXPERTS * blocks * CAP,), blocks * assigned, dtype=jnp.int32)
    table = table.at[position.reshape(-1)].set(global_id.reshape(-1))
    table = table.reshape(EXPERTS, blocks * CAP)
    tokens_pad = jnp.concatenate([tokens, jnp.zeros((1, D), jnp.bfloat16)], axis=0)
    cot_pad = jnp.concatenate([cotangent, jnp.zeros((1, D), jnp.bfloat16)], axis=0)
    weight_pad = jnp.concatenate([route_weight.reshape(-1), jnp.zeros((1,), jnp.float32)], axis=0)

    def one_expert(packed):
        index, table_row = packed
        return expert_pass(index, table_row, tokens_pad, cot_pad, weight_pad, w_gate, w_up, w_down)

    parts, grads = lax.map(one_expert, (jnp.arange(EXPERTS, dtype=jnp.int32), table))
    flat_parts = parts.reshape(EXPERTS * blocks * CAP, D)
    per_assign = flat_parts[position.reshape(-1)]
    token_grad = jnp.sum(per_assign.reshape(TOKENS, TOPK, D).astype(jnp.float32), axis=1).astype(jnp.bfloat16)
    down_grad = jnp.transpose(grads, (1, 0, 2))
    return token_grad, down_grad
```

```python
import functools

import jax
import jax.numpy as jnp
from jax import lax
from jax.experimental import pallas as pl
from jax.experimental.pallas import tpu as pltpu
from jax.sharding import PartitionSpec as P

CAP = 3
LANE = 128
BF16 = jnp.bfloat16
F32 = jnp.float32

VMEM = pl.BlockSpec(memory_space=pltpu.VMEM)
SMEM = pl.BlockSpec(memory_space=pltpu.SMEM)
HBM = pl.BlockSpec(memory_space=pltpu.HBM)


def mm(a, b, ca=1, cb=0):
    return lax.dot_general(a, b, (((ca,), (cb,)), ((), ())), preferred_element_type=F32)


def slots_of(ids_row, peers):
    n = ids_row.shape[1]
    across = jnp.broadcast_to(ids_row, (n, n))
    down = across.T
    row = lax.broadcasted_iota(jnp.int32, (n, n), 0)
    col = lax.broadcasted_iota(jnp.int32, (n, n), 1)
    earlier = jnp.where((across == down) & (row < col), 1.0, 0.0).astype(F32)
    rank = jnp.sum(earlier, axis=0, keepdims=True).astype(jnp.int32)
    return rank * peers + ids_row


def placing_of(ids_row, peers):
    n = ids_row.shape[1]
    lines = lax.broadcasted_iota(jnp.int32, (CAP * peers, n), 0)
    return jnp.where(lines == slots_of(ids_row, peers), 1.0, 0.0).astype(BF16)


def lanes(q, count=1):
    return slice(q * LANE, (q + count) * LANE)


def pack_kernel(
    peers, ids_ref, weight_ref, tok_hbm, cot_hbm, out_hbm, tok, cot, out, scr, sems
):
    copies = [
        pltpu.make_async_copy(tok_hbm, tok, sems.at[0]),
        pltpu.make_async_copy(cot_hbm, cot, sems.at[1]),
    ]
    for copy in copies:
        copy.start()
    n, width = tok.shape
    chunks = width // LANE
    placing = placing_of(ids_ref[...], peers)
    weight = jnp.broadcast_to(weight_ref[...], (n, n)).T[:, :1]
    sent = []
    for which in range(2):
        copies[which].wait()
        for c in range(0, chunks, 2):
            if which == 0:
                rows = tok[:, lanes(c, 2)]
            else:
                rows = (weight * cot[:, lanes(c, 2)].astype(F32)).astype(BF16)
            placed = mm(placing, rows)
            for s in range(CAP):
                for h in range(2):
                    scr[CAP * which + s, pl.ds(c + h, peers, stride=chunks), :] = placed[
                        s * peers : (s + 1) * peers, lanes(h)
                    ]
        for q in range(CAP * which, CAP * which + CAP):
            out[which, :, :, lanes(q % CAP)] = (
                scr[q].reshape(peers, chunks, LANE).astype(BF16)
            )
        copy = pltpu.make_async_copy(
            out.at[which], out_hbm.at[:, :, pl.ds(which * CAP * LANE, CAP * LANE)], sems.at[2 + which]
        )
        copy.start()
        sent.append(copy)
    for copy in sent:
        copy.wait()


def to_rows(got, scr):
    peers, chunks, _ = got.shape
    for s in range(CAP):
        scr[s] = got[:, :, lanes(s)].astype(F32).reshape(peers * chunks, LANE)
    for s in range(CAP):
        for c in range(chunks):
            yield slice(s * peers, (s + 1) * peers), c, scr[s, pl.ds(c, peers, stride=chunks), :]


def expert_kernel(
    core_ref, got_hbm, wg_hbm, wu_hbm, down_hbm,
    part_hbm, keep_hbm, send_hbm,
    got, wg, wu, down, scr, rows, cot, own, other, keep, send, part, sems,
):
    sources = [
        (got_hbm.at[:, :, pl.ds(0, CAP * LANE)], got.at[0]),
        (got_hbm.at[:, :, pl.ds(CAP * LANE, CAP * LANE)], got.at[1]),
        (wg_hbm, wg),
        (wu_hbm, wu),
        (down_hbm, down),
    ]
    copies = [
        pltpu.make_async_copy(a, b, sems.at[i]) for i, (a, b) in enumerate(sources)
    ]
    for copy in copies:
        copy.start()
    peers, chunks, _ = part.shape
    first = core_ref[0] == 0
    copies[0].wait()
    for lines, c, value in to_rows(got.at[0], scr):
        rows[lines, lanes(c)] = value.astype(BF16)
    copies[2].wait()
    gate = mm(rows[...], wg[...])
    sig = jax.nn.sigmoid(gate)
    copies[3].wait()
    up = mm(rows[...], wu[...])
    hidden = (gate * sig * up).astype(BF16)
    copies[1].wait()
    even = None
    for lines, c, value in to_rows(got.at[1], scr):
        cot[lines, lanes(c)] = value.astype(BF16)
        if c % 2 == 0:
            even = value
        else:
            own[lines, lanes(c // 2)] = jnp.where(first, even, value).astype(BF16)
            other[lines, lanes(c // 2)] = jnp.where(first, value, even).astype(BF16)
    sent = []
    for i, (source, target, target_hbm) in enumerate(
        ((other, send, send_hbm), (own, keep, keep_hbm))
    ):
        for b in range(chunks // 2):
            target[b] = mm(source[:, lanes(b)], hidden, 0, 0).astype(BF16)
        copy = pltpu.make_async_copy(target, target_hbm, sems.at[5 + i])
        copy.start()
        sent.append(copy)
    copies[4].wait()
    grad = mm(cot[...], down[...])
    gate_grad = (grad * up * sig * (1.0 + gate * (1.0 - sig))).astype(BF16)
    up_grad = (grad * (gate * sig)).astype(BF16)
    for c in range(0, chunks, 2):
        at = lanes(c, 2)
        value = mm(gate_grad, wg[at, :], 1, 1) + mm(up_grad, wu[at, :], 1, 1)
        for s in range(CAP):
            for h in range(2):
                scr[s, pl.ds(c + h, peers, stride=chunks), :] = value[
                    s * peers : (s + 1) * peers, lanes(h)
                ]
    for s in range(CAP):
        part[:, :, lanes(s)] = scr[s].reshape(peers, chunks, LANE).astype(BF16)
    copy = pltpu.make_async_copy(part, part_hbm, sems.at[7])
    copy.start()
    sent.append(copy)
    for copy in sent:
        copy.wait()


def collect_kernel(peers, ids_ref, got_hbm, out_ref, got, scr, rows, sem):
    copy = pltpu.make_async_copy(got_hbm, got, sem)
    copy.start()
    placing = placing_of(ids_ref[...], peers)
    copy.wait()
    for lines, c, value in to_rows(got, scr):
        rows[lines, lanes(c)] = value.astype(BF16)
    out_ref[...] = mm(placing, rows[...], 0, 0).astype(BF16)


def call(kernel, out_shape, in_specs, out_specs, scratch, limit, flops, moved, name):
    return pl.pallas_call(
        kernel,
        out_shape=out_shape,
        in_specs=in_specs,
        out_specs=out_specs,
        scratch_shapes=scratch,
        compiler_params=pltpu.CompilerParams(vmem_limit_bytes=limit << 20),
        cost_estimate=pl.CostEstimate(flops=flops, bytes_accessed=moved, transcendentals=0),
        name=name,
    )


def reduce_features(keep, send):
    ranks = lax.axis_size("dp")
    chips = ranks // 2
    me = lax.axis_index("dp")
    z = me // 2
    step = 1 - 2 * (me % 2)
    swapped = lax.ppermute(send, "dp", [(d, d ^ 1) for d in range(ranks)])
    onward = [
        (d, (d // 2 + 1 - 2 * (d % 2)) % chips * 2 + d % 2) for d in range(ranks)
    ]

    def term(k):
        at = lax.rem(z - k * step + 2 * chips, chips)
        mine = lax.dynamic_index_in_dim(keep, at, 0, keepdims=False)
        theirs = lax.dynamic_index_in_dim(swapped, at, 0, keepdims=False)
        return mine.astype(F32) + theirs.astype(F32)

    total = term(1)
    for k in range(1, chips):
        arrived = lax.ppermute(total.astype(BF16), "dp", onward)
        total = term(k + 1) + arrived.astype(F32)
    return total


def on_device(tokens, cotangent, expert_ids, route_weight, w_gate, w_up, w_down):
    n, width = tokens.shape
    peers = lax.axis_size("expert")
    ranks = lax.axis_size("dp")
    hidden = w_gate.shape[2]
    chunks = width // LANE
    slots = CAP * peers
    product = 2 * slots * width * hidden
    core = (lax.axis_index("dp") % 2).astype(jnp.int32).reshape(1)
    ids = expert_ids.reshape(1, n)
    weight = route_weight.reshape(1, n)
    wg = w_gate.reshape(width, hidden)
    wu = w_up.reshape(width, hidden)
    full_down = lax.all_gather(w_down.reshape(width // ranks, hidden), "dp", axis=0, tiled=True)

    shape = jax.ShapeDtypeStruct
    packed = call(
        functools.partial(pack_kernel, peers),
        shape((peers, chunks, 2 * CAP * LANE), BF16),
        [VMEM, VMEM, HBM, HBM],
        HBM,
        [
            pltpu.VMEM((n, width), BF16),
            pltpu.VMEM((n, width), BF16),
            pltpu.VMEM((2, peers, chunks, CAP * LANE), BF16),
            pltpu.VMEM((2 * CAP, peers * chunks, LANE), F32),
            pltpu.SemaphoreType.DMA((4,)),
        ],
        58, 4 * slots * n * width, 4 << 20, "pack",
    )(ids, weight, tokens, cotangent)
    got = lax.all_to_all(packed, "expert", split_axis=0, concat_axis=0, tiled=True)

    part, keep, send = call(
        expert_kernel,
        (
            shape((peers, chunks, CAP * LANE), BF16),
            shape((chunks // 2, LANE, hidden), BF16),
            shape((chunks // 2, LANE, hidden), BF16),
        ),
        [SMEM, HBM, HBM, HBM, HBM],
        (HBM, HBM, HBM),
        [
            pltpu.VMEM((2, peers, chunks, CAP * LANE), BF16),
            pltpu.VMEM((width, hidden), BF16),
            pltpu.VMEM((width, hidden), BF16),
            pltpu.VMEM((width, hidden), BF16),
            pltpu.VMEM((CAP, peers * chunks, LANE), F32),
            pltpu.VMEM((slots, width), BF16),
            pltpu.VMEM((slots, width), BF16),
            pltpu.VMEM((slots, width // 2), BF16),
            pltpu.VMEM((slots, width // 2), BF16),
            pltpu.VMEM((chunks // 2, LANE, hidden), BF16),
            pltpu.VMEM((chunks // 2, LANE, hidden), BF16),
            pltpu.VMEM((peers, chunks, CAP * LANE), BF16),
            pltpu.SemaphoreType.DMA((8,)),
        ],
        48, 6 * product, 16 << 20, "expert",
    )(core, got, wg, wu, full_down)

    down_part = reduce_features(keep, send)
    returned = lax.all_to_all(part, "expert", split_axis=0, concat_axis=0, tiled=True)

    token_grad = call(
        functools.partial(collect_kernel, peers),
        shape((n, width), BF16),
        [VMEM, HBM],
        VMEM,
        [
            pltpu.VMEM((peers, chunks, CAP * LANE), BF16),
            pltpu.VMEM((CAP, peers * chunks, LANE), F32),
            pltpu.VMEM((slots, width), BF16),
            pltpu.SemaphoreType.DMA,
        ],
        16, 2 * slots * n * width, 2 << 20, "collect",
    )(ids, returned)
    return (token_grad, down_part.reshape(w_down.shape))


def solution(mesh):
    in_specs = (
        P(("expert", "dp"), None),
        P(("expert", "dp"), None),
        P(("expert", "dp"), None),
        P(("expert", "dp"), None),
        P("expert", None, None),
        P("expert", None, None),
        P("dp", "expert", None),
    )
    out_specs = (P(("expert", "dp"), None), P("dp", "expert", None))
    return jax.shard_map(
        on_device, mesh=mesh, in_specs=in_specs, out_specs=out_specs, check_vma=False
    )
```

```python
import functools

import jax
import jax.numpy as jnp
from jax import lax
from jax.experimental import pallas as pl
from jax.experimental.pallas import tpu as pltpu
from jax.sharding import Mesh, PartitionSpec as P

CAP = 3
LANE = 128
BF16 = jnp.bfloat16
F32 = jnp.float32

VMEM = pl.BlockSpec(memory_space=pltpu.VMEM)
SMEM = pl.BlockSpec(memory_space=pltpu.SMEM)
HBM = pl.BlockSpec(memory_space=pltpu.HBM)


def mm(a, b, ca=1, cb=0):
    return lax.dot_general(a, b, (((ca,), (cb,)), ((), ())), preferred_element_type=F32)


def slots_of(ids_row, peers):
    n = ids_row.shape[1]
    across = jnp.broadcast_to(ids_row, (n, n))
    down = across.T
    row = lax.broadcasted_iota(jnp.int32, (n, n), 0)
    col = lax.broadcasted_iota(jnp.int32, (n, n), 1)
    earlier = jnp.where((across == down) & (row < col), 1.0, 0.0).astype(F32)
    rank = jnp.sum(earlier, axis=0, keepdims=True).astype(jnp.int32)
    return rank * peers + ids_row


def placing_of(ids_row, peers):
    n = ids_row.shape[1]
    lines = lax.broadcasted_iota(jnp.int32, (CAP * peers, n), 0)
    return jnp.where(lines == slots_of(ids_row, peers), 1.0, 0.0).astype(BF16)


def lanes(q, count=1):
    return slice(q * LANE, (q + count) * LANE)


def pack_kernel(
    peers, ids_ref, weight_ref, tok_hbm, cot_hbm, out_hbm, tok, cot, out, scr, sems
):
    copies = [
        pltpu.make_async_copy(tok_hbm, tok, sems.at[0]),
        pltpu.make_async_copy(cot_hbm, cot, sems.at[1]),
    ]
    for copy in copies:
        copy.start()
    n, width = tok.shape
    chunks = width // LANE
    placing = placing_of(ids_ref[...], peers)
    weight = jnp.broadcast_to(weight_ref[...], (n, n)).T[:, :1]
    sent = []
    for which in range(2):
        copies[which].wait()
        for c in range(0, chunks, 2):
            if which == 0:
                rows = tok[:, lanes(c, 2)]
            else:
                rows = (weight * cot[:, lanes(c, 2)].astype(F32)).astype(BF16)
            placed = mm(placing, rows)
            for s in range(CAP):
                for h in range(2):
                    scr[CAP * which + s, pl.ds(c + h, peers, stride=chunks), :] = placed[
                        s * peers : (s + 1) * peers, lanes(h)
                    ]
        for q in range(CAP * which, CAP * which + CAP):
            out[which, :, :, lanes(q % CAP)] = (
                scr[q].reshape(peers, chunks, LANE).astype(BF16)
            )
        copy = pltpu.make_async_copy(
            out.at[which], out_hbm.at[:, :, pl.ds(which * CAP * LANE, CAP * LANE)], sems.at[2 + which]
        )
        copy.start()
        sent.append(copy)
    for copy in sent:
        copy.wait()


def to_rows(got, scr):
    peers, chunks, _ = got.shape
    for s in range(CAP):
        scr[s] = got[:, :, lanes(s)].astype(F32).reshape(peers * chunks, LANE)
    for s in range(CAP):
        for c in range(chunks):
            yield slice(s * peers, (s + 1) * peers), c, scr[s, pl.ds(c, peers, stride=chunks), :]


def start_all(pairs, sems, base=0):
    copies = [
        pltpu.make_async_copy(source, target, sems.at[base + i])
        for i, (source, target) in enumerate(pairs)
    ]
    for copy in copies:
        copy.start()
    return copies


def forward_kernel(
    got_hbm, wg_hbm, wu_hbm,
    terms_hbm, gate_hbm, up_hbm, cot_hbm,
    got, wg, wu, scr, rows, cot, gate, up, terms, sems,
):
    copies = start_all(
        [
            (got_hbm.at[:, :, pl.ds(0, CAP * LANE)], got.at[0]),
            (wg_hbm, wg),
            (wu_hbm, wu),
            (got_hbm.at[:, :, pl.ds(CAP * LANE, CAP * LANE)], got.at[1]),
        ],
        sems,
    )
    chunks = got.shape[2]
    copies[0].wait()
    for lines, c, value in to_rows(got.at[0], scr):
        rows[lines, lanes(c)] = value.astype(BF16)
    copies[1].wait()
    gate_value = mm(rows[...], wg[...])
    gate[...] = gate_value
    copies[2].wait()
    up_value = mm(rows[...], wu[...])
    up[...] = up_value
    hidden = (gate_value * jax.nn.sigmoid(gate_value) * up_value).astype(BF16)
    sent = start_all([(gate, gate_hbm), (up, up_hbm)], sems, 4)
    copies[3].wait()
    for lines, c, value in to_rows(got.at[1], scr):
        cot[lines, lanes(c)] = value.astype(BF16)
    sent += start_all([(cot, cot_hbm)], sems, 6)
    half = chunks // 2 * LANE
    for part in range(2):
        for b in range(part * chunks // 2, (part + 1) * chunks // 2, 2):
            at = lanes(b, 2)
            terms[at, :] = mm(cot[:, at], hidden, 0, 0).astype(BF16)
        at = pl.ds(part * half, half)
        sent += start_all([(terms.at[at, :], terms_hbm.at[at, :])], sems, 7 + part)
    for copy in sent:
        copy.wait()


def backward_kernel(
    gate_hbm, up_hbm, cot_hbm, down_hbm, wg_hbm, wu_hbm,
    part_hbm,
    gate, up, cot, down, wg, wu, scr, part, sems,
):
    copies = start_all(
        [
            (cot_hbm, cot),
            (down_hbm, down),
            (gate_hbm, gate),
            (up_hbm, up),
            (wg_hbm, wg),
            (wu_hbm, wu),
        ],
        sems,
    )
    peers, chunks, _ = part.shape
    copies[0].wait()
    copies[1].wait()
    grad = mm(cot[...], down[...])
    copies[2].wait()
    copies[3].wait()
    v = gate[...]
    sig = jax.nn.sigmoid(v)
    gate_grad = (grad * up[...] * sig * (1.0 + v * (1.0 - sig))).astype(BF16)
    up_grad = (grad * (v * sig)).astype(BF16)
    copies[4].wait()
    copies[5].wait()
    for c in range(0, chunks, 2):
        at = lanes(c, 2)
        value = mm(gate_grad, wg[at, :], 1, 1) + mm(up_grad, wu[at, :], 1, 1)
        for s in range(CAP):
            for h in range(2):
                scr[s, pl.ds(c + h, peers, stride=chunks), :] = value[
                    s * peers : (s + 1) * peers, lanes(h)
                ]
    for s in range(CAP):
        part[:, :, lanes(s)] = scr[s].reshape(peers, chunks, LANE).astype(BF16)
    for copy in start_all([(part, part_hbm)], sems, 6):
        copy.wait()


def collect_kernel(peers, ids_ref, got_hbm, out_ref, got, scr, rows, sem):
    copy = pltpu.make_async_copy(got_hbm, got, sem)
    copy.start()
    placing = placing_of(ids_ref[...], peers)
    copy.wait()
    for lines, c, value in to_rows(got, scr):
        rows[lines, lanes(c)] = value.astype(BF16)
    out_ref[...] = mm(placing, rows[...], 0, 0).astype(BF16)


def call(kernel, out_shape, in_specs, out_specs, scratch, limit, flops, moved, name):
    return pl.pallas_call(
        kernel,
        out_shape=out_shape,
        in_specs=in_specs,
        out_specs=out_specs,
        scratch_shapes=scratch,
        compiler_params=pltpu.CompilerParams(vmem_limit_bytes=limit << 20),
        cost_estimate=pl.CostEstimate(flops=flops, bytes_accessed=moved, transcendentals=0),
        name=name,
    )


def reduce_features(terms):
    over_z = lax.psum_scatter(terms, "z", scatter_dimension=0, tiled=True)
    both = over_z.reshape(2, LANE, terms.shape[1])
    core = lax.axis_index("core")
    mine = lax.dynamic_index_in_dim(both, core, 0, keepdims=False)
    other = lax.dynamic_index_in_dim(both, 1 - core, 0, keepdims=False)
    arrived = lax.ppermute(other, "core", [(0, 1), (1, 0)])
    return mine.astype(F32) + arrived.astype(F32)


def on_device(tokens, cotangent, expert_ids, route_weight, w_gate, w_up, w_down):
    n, width = tokens.shape
    peers = lax.axis_size("expert")
    ranks = lax.axis_size("z") * 2
    hidden = w_gate.shape[2]
    chunks = width // LANE
    slots = CAP * peers
    product = 2 * slots * width * hidden
    ids = expert_ids.reshape(1, n)
    weight = route_weight.reshape(1, n)
    wg = w_gate.reshape(width, hidden)
    wu = w_up.reshape(width, hidden)
    full_down = lax.all_gather(w_down.reshape(width // ranks, hidden), ("z", "core"), axis=0, tiled=True)

    shape = jax.ShapeDtypeStruct
    packed = call(
        functools.partial(pack_kernel, peers),
        shape((peers, chunks, 2 * CAP * LANE), BF16),
        [VMEM, VMEM, HBM, HBM],
        HBM,
        [
            pltpu.VMEM((n, width), BF16),
            pltpu.VMEM((n, width), BF16),
            pltpu.VMEM((2, peers, chunks, CAP * LANE), BF16),
            pltpu.VMEM((2 * CAP, peers * chunks, LANE), F32),
            pltpu.SemaphoreType.DMA((4,)),
        ],
        58, 4 * slots * n * width, 4 << 20, "pack",
    )(ids, weight, tokens, cotangent)
    got = lax.all_to_all(packed, "expert", split_axis=0, concat_axis=0, tiled=True)

    weights = pltpu.VMEM((width, hidden), BF16)
    inner = pltpu.VMEM((slots, hidden), F32)
    terms, gate, up, cot = call(
        forward_kernel,
        (
            shape((width, hidden), BF16),
            shape((slots, hidden), F32),
            shape((slots, hidden), F32),
            shape((slots, width), BF16),
        ),
        [HBM] * 3,
        (HBM,) * 4,
        [
            pltpu.VMEM((2, peers, chunks, CAP * LANE), BF16),
            weights,
            weights,
            pltpu.VMEM((CAP, peers * chunks, LANE), F32),
            pltpu.VMEM((slots, width), BF16),
            pltpu.VMEM((slots, width), BF16),
            inner,
            inner,
            weights,
            pltpu.SemaphoreType.DMA((9,)),
        ],
        48, 3 * product, 14 << 20, "forward",
    )(got, wg, wu)

    part = call(
        backward_kernel,
        shape((peers, chunks, CAP * LANE), BF16),
        [HBM] * 6,
        HBM,
        [
            inner,
            inner,
            pltpu.VMEM((slots, width), BF16),
            weights,
            weights,
            weights,
            pltpu.VMEM((CAP, peers * chunks, LANE), F32),
            pltpu.VMEM((peers, chunks, CAP * LANE), BF16),
            pltpu.SemaphoreType.DMA((7,)),
        ],
        58, 3 * product, 14 << 20, "backward",
    )(gate, up, cot, full_down, wg, wu)

    down_part = reduce_features(terms)
    returned = lax.all_to_all(part, "expert", split_axis=0, concat_axis=0, tiled=True)

    token_grad = call(
        functools.partial(collect_kernel, peers),
        shape((n, width), BF16),
        [VMEM, HBM],
        VMEM,
        [
            pltpu.VMEM((peers, chunks, CAP * LANE), BF16),
            pltpu.VMEM((CAP, peers * chunks, LANE), F32),
            pltpu.VMEM((slots, width), BF16),
            pltpu.SemaphoreType.DMA,
        ],
        16, 2 * slots * n * width, 2 << 20, "collect",
    )(ids, returned)
    return (token_grad, down_part.reshape(w_down.shape))


def solution(mesh):
    ranks = mesh.shape["dp"]
    split = Mesh(
        mesh.devices.reshape(mesh.shape["expert"], ranks // 2, 2), ("expert", "z", "core")
    )
    tokens = P(("expert", "z", "core"), None)
    experts = P("expert", None, None)
    features = P(("z", "core"), "expert", None)
    return jax.shard_map(
        on_device,
        mesh=split,
        in_specs=(tokens, tokens, tokens, tokens, experts, experts, features),
        out_specs=(tokens, features),
        check_vma=False,
    )
```

```python
import functools

import jax
import jax.numpy as jnp
from jax import lax
from jax.experimental import pallas as pl
from jax.experimental.pallas import tpu as pltpu
from jax.sharding import Mesh, PartitionSpec as P

CAP = 3
LANE = 128
NEAR = (0, -1, 1, -3, 3, -2, -4, 2)
FOLD = (-2, -4, 2, 3, -3, -1, 1, 0)
BF16 = jnp.bfloat16
F32 = jnp.float32

VMEM = pl.BlockSpec(memory_space=pltpu.VMEM)
SMEM = pl.BlockSpec(memory_space=pltpu.SMEM)
HBM = pl.BlockSpec(memory_space=pltpu.HBM)


def mm(a, b, ca=1, cb=0):
    return lax.dot_general(a, b, (((ca,), (cb,)), ((), ())), preferred_element_type=F32)


def slots_of(ids_row, peers):
    n = ids_row.shape[1]
    across = jnp.broadcast_to(ids_row, (n, n))
    down = across.T
    row = lax.broadcasted_iota(jnp.int32, (n, n), 0)
    col = lax.broadcasted_iota(jnp.int32, (n, n), 1)
    earlier = jnp.where((across == down) & (row < col), 1.0, 0.0).astype(F32)
    rank = jnp.sum(earlier, axis=0, keepdims=True).astype(jnp.int32)
    return rank * peers + ids_row


def placing_of(ids_row, peers):
    n = ids_row.shape[1]
    lines = lax.broadcasted_iota(jnp.int32, (CAP * peers, n), 0)
    return jnp.where(lines == slots_of(ids_row, peers), 1.0, 0.0).astype(BF16)


def lanes(q, count=1):
    return slice(q * LANE, (q + count) * LANE)


def start_all(pairs, sems, base=0):
    copies = [
        pltpu.make_async_copy(source, target, sems.at[base + i])
        for i, (source, target) in enumerate(pairs)
    ]
    for copy in copies:
        copy.start()
    return copies


def pack_kernel(
    peers, ids_ref, weight_ref, tok_hbm, cot_hbm, own_hbm,
    out_hbm, passed_hbm,
    tok, cot, out, scr, sems,
):
    copies = start_all([(tok_hbm, tok), (cot_hbm, cot), (own_hbm, passed_hbm)], sems)
    n, width = tok.shape
    chunks = width // LANE
    placing = placing_of(ids_ref[...], peers)
    weight = jnp.broadcast_to(weight_ref[...], (n, n)).T[:, :1]
    sent = copies[2:]
    for which in range(2):
        copies[which].wait()
        for c in range(0, chunks, 2):
            if which == 0:
                rows = tok[:, lanes(c, 2)]
            else:
                rows = (weight * cot[:, lanes(c, 2)].astype(F32)).astype(BF16)
            placed = mm(placing, rows)
            for s in range(CAP):
                for h in range(2):
                    scr[CAP * which + s, pl.ds(c + h, peers, stride=chunks), :] = placed[
                        s * peers : (s + 1) * peers, lanes(h)
                    ]
        for q in range(CAP * which, CAP * which + CAP):
            out[which, :, :, lanes(q % CAP)] = (
                scr[q].reshape(peers, chunks, LANE).astype(BF16)
            )
        copy = pltpu.make_async_copy(
            out.at[which], out_hbm.at[:, :, pl.ds(which * CAP * LANE, CAP * LANE)], sems.at[3 + which]
        )
        copy.start()
        sent.append(copy)
    for copy in sent:
        copy.wait()


def to_rows(got, scr):
    peers, chunks, _ = got.shape
    for s in range(CAP):
        scr[s] = got[:, :, lanes(s)].astype(F32).reshape(peers * chunks, LANE)
    for s in range(CAP):
        for c in range(chunks):
            yield slice(s * peers, (s + 1) * peers), c, scr[s, pl.ds(c, peers, stride=chunks), :]


def expert_kernel(
    place_ref, got_hbm, wg_hbm, wu_hbm, first_hbm, rest_hbm, first_other_hbm, rest_other_hbm,
    part_hbm, send_hbm, keep_hbm,
    got, wg, wu, down, scr, rows, cot, own, other, send, keep, part, sems,
):
    z, core = place_ref[0], place_ref[1]
    copies = start_all(
        [
            (got_hbm.at[:, :, pl.ds(0, CAP * LANE)], got.at[0]),
            (wg_hbm, wg),
            (wu_hbm, wu),
            (got_hbm.at[:, :, pl.ds(CAP * LANE, CAP * LANE)], got.at[1]),
        ],
        sems,
    )
    near = first_hbm.shape[0]
    chips = near + rest_hbm.shape[0]
    gathered = []
    for i, step in enumerate(NEAR):
        chip = lax.rem(z + (step + chips), chips)
        mine, theirs = (first_hbm, first_other_hbm) if i < near else (rest_hbm, rest_other_hbm)
        at = i if i < near else i - near
        gathered.append((mine.at[at], down.at[chip * 2 + core]))
        gathered.append((theirs.at[at], down.at[chip * 2 + 1 - core]))
    arriving = start_all(gathered, sems, 7)
    peers, chunks, _ = part.shape
    first = core == 0
    copies[0].wait()
    for lines, c, value in to_rows(got.at[0], scr):
        rows[lines, lanes(c)] = value.astype(BF16)
    copies[1].wait()
    gate = mm(rows[...], wg[...])
    sig = jax.nn.sigmoid(gate)
    copies[2].wait()
    up = mm(rows[...], wu[...])
    hidden = (gate * sig * up).astype(BF16)
    copies[3].wait()
    even = None
    for lines, c, value in to_rows(got.at[1], scr):
        cot[lines, lanes(c)] = value.astype(BF16)
        if c % 2 == 0:
            even = value
        else:
            own[lines, lanes(c // 2)] = jnp.where(first, even, value).astype(BF16)
            other[lines, lanes(c // 2)] = jnp.where(first, value, even).astype(BF16)
    sent = []
    for i, (source, target, target_hbm) in enumerate(
        ((other, send, send_hbm), (own, keep, keep_hbm))
    ):
        for b in range(0, chunks // 2, 2):
            value = mm(source[:, lanes(b, 2)], hidden, 0, 0).astype(BF16)
            target[b] = value[:LANE]
            target[b + 1] = value[LANE:]
        sent += start_all([(target, target_hbm)], sems, 4 + i)
    for copy in arriving:
        copy.wait()
    grad = mm(cot[...], down[...].reshape(wg.shape))
    gate_grad = (grad * up * sig * (1.0 + gate * (1.0 - sig))).astype(BF16)
    up_grad = (grad * (gate * sig)).astype(BF16)
    for c in range(0, chunks, 2):
        at = lanes(c, 2)
        value = mm(gate_grad, wg[at, :], 1, 1) + mm(up_grad, wu[at, :], 1, 1)
        for s in range(CAP):
            for h in range(2):
                scr[s, pl.ds(c + h, peers, stride=chunks), :] = value[
                    s * peers : (s + 1) * peers, lanes(h)
                ]
    for s in range(CAP):
        part[:, :, lanes(s)] = scr[s].reshape(peers, chunks, LANE).astype(BF16)
    sent += start_all([(part, part_hbm)], sems, 6)
    for copy in sent:
        copy.wait()


def fold_kernel(
    place_ref, keep_hbm, swapped_hbm,
    above_ref, below_ref, far_ref, outer_ref, inner_ref, under_ref, last_ref,
    kept, came, sems,
):
    z = place_ref[0]
    chips = keep_hbm.shape[0]
    copies = []
    for i, step in enumerate(FOLD):
        chip = lax.rem(z + (step + chips), chips)
        copies.append(
            start_all(
                [(keep_hbm.at[chip], kept.at[i]), (swapped_hbm.at[chip], came.at[i])], sems, 2 * i
            )
        )
    targets = (
        above_ref.at[0], above_ref.at[1], below_ref, far_ref,
        outer_ref, inner_ref, under_ref, last_ref,
    )
    for i, target in enumerate(targets):
        for copy in copies[i]:
            copy.wait()
        target[...] = (kept[i].astype(F32) + came[i].astype(F32)).astype(target.dtype)


def collect_kernel(peers, ids_ref, got_hbm, out_ref, got, scr, rows, sem):
    copy = pltpu.make_async_copy(got_hbm, got, sem)
    copy.start()
    placing = placing_of(ids_ref[...], peers)
    copy.wait()
    for lines, c, value in to_rows(got, scr):
        rows[lines, lanes(c)] = value.astype(BF16)
    out_ref[...] = mm(placing, rows[...], 0, 0).astype(BF16)


def call(kernel, out_shape, in_specs, out_specs, scratch, limit, flops, moved, name):
    return pl.pallas_call(
        kernel,
        out_shape=out_shape,
        in_specs=in_specs,
        out_specs=out_specs,
        scratch_shapes=scratch,
        compiler_params=pltpu.CompilerParams(vmem_limit_bytes=limit << 20),
        cost_estimate=pl.CostEstimate(flops=flops, bytes_accessed=moved, transcendentals=0),
        name=name,
    )


def over_core(x):
    return lax.ppermute(x, "core", [(0, 1), (1, 0)])


def round_z(x, step):
    chips = lax.axis_size("z")
    return lax.ppermute(x, "z", [(j, (j + step) % chips) for j in range(chips)])


def gather_features(own):
    m1, p1, m3, p3 = round_z(own, 1), round_z(own, -1), round_z(own, 3), round_z(own, -3)
    m2, m4 = jnp.split(round_z(jnp.concatenate([m1, m3]), 1), 2)
    p2 = round_z(p1, -1)
    first = jnp.stack([own, m1, p1, m3, p3])
    rest = jnp.stack([m2, m4, p2])
    return first, rest, over_core(first), over_core(rest)


def reduce_features(place, keep, swapped):
    blocks, lines, hidden = keep.shape
    narrow = jax.ShapeDtypeStruct((lines, hidden), BF16)
    wide = jax.ShapeDtypeStruct((lines, hidden), F32)
    both = jax.ShapeDtypeStruct((2, lines, hidden), BF16)
    pair, low, far_low, outer, inner, under, total = call(
        fold_kernel,
        (both, narrow, narrow, wide, wide, wide, wide),
        [SMEM, HBM, HBM],
        (VMEM,) * 7,
        [
            pltpu.VMEM(keep.shape, BF16),
            pltpu.VMEM(keep.shape, BF16),
            pltpu.SemaphoreType.DMA((2 * blocks,)),
        ],
        24, keep.size, 6 * keep.size, "fold",
    )(place, keep, swapped)
    above = round_z(pair, -1)
    below = round_z(low, 1)
    far_below = round_z(far_low, 3)
    far_above = round_z((outer + above[1].astype(F32)).astype(BF16), -3)
    near_above = round_z((inner + above[0].astype(F32)).astype(BF16), -1)
    near_below = round_z((under + below.astype(F32)).astype(BF16), 1)
    for arrived in (near_above, far_above, near_below, far_below):
        total = total + arrived.astype(F32)
    return total


def on_device(tokens, cotangent, expert_ids, route_weight, w_gate, w_up, w_down):
    n, width = tokens.shape
    peers = lax.axis_size("expert")
    ranks = lax.axis_size("z") * 2
    hidden = w_gate.shape[2]
    chunks = width // LANE
    slots = CAP * peers
    product = 2 * slots * width * hidden
    ids = expert_ids.reshape(1, n)
    weight = route_weight.reshape(1, n)
    wg = w_gate.reshape(width, hidden)
    wu = w_up.reshape(width, hidden)
    place = jnp.stack([lax.axis_index("z"), lax.axis_index("core")]).astype(jnp.int32)
    own = w_down.reshape(width // ranks, hidden)

    shape = jax.ShapeDtypeStruct
    packed, own = call(
        functools.partial(pack_kernel, peers),
        (shape((peers, chunks, 2 * CAP * LANE), BF16), shape(own.shape, BF16)),
        [VMEM, VMEM, HBM, HBM, HBM],
        (HBM, HBM),
        [
            pltpu.VMEM((n, width), BF16),
            pltpu.VMEM((n, width), BF16),
            pltpu.VMEM((2, peers, chunks, CAP * LANE), BF16),
            pltpu.VMEM((2 * CAP, peers * chunks, LANE), F32),
            pltpu.SemaphoreType.DMA((5,)),
        ],
        58, 4 * slots * n * width, 4 << 20, "pack",
    )(ids, weight, tokens, cotangent, own)
    got = lax.all_to_all(packed, "expert", split_axis=0, concat_axis=0, tiled=True)
    gathered = gather_features(own)

    weights = pltpu.VMEM((width, hidden), BF16)
    features = pltpu.VMEM((chunks // 2, LANE, hidden), BF16)
    part, send, keep = call(
        expert_kernel,
        (
            shape((peers, chunks, CAP * LANE), BF16),
            shape((chunks // 2, LANE, hidden), BF16),
            shape((chunks // 2, LANE, hidden), BF16),
        ),
        [SMEM] + [HBM] * 7,
        (HBM,) * 3,
        [
            pltpu.VMEM((2, peers, chunks, CAP * LANE), BF16),
            weights,
            weights,
            pltpu.VMEM((chunks, LANE, hidden), BF16),
            pltpu.VMEM((CAP, peers * chunks, LANE), F32),
            pltpu.VMEM((slots, width), BF16),
            pltpu.VMEM((slots, width), BF16),
            pltpu.VMEM((slots, width // 2), BF16),
            pltpu.VMEM((slots, width // 2), BF16),
            features,
            features,
            pltpu.VMEM((peers, chunks, CAP * LANE), BF16),
            pltpu.SemaphoreType.DMA((7 + chunks,)),
        ],
        58, 6 * product, 18 << 20, "expert",
    )(place, got, wg, wu, *gathered)
    swapped = over_core(send)
    down_part = reduce_features(place, keep, swapped)
    returned = lax.all_to_all(part, "expert", split_axis=0, concat_axis=0, tiled=True)

    token_grad = call(
        functools.partial(collect_kernel, peers),
        shape((n, width), BF16),
        [VMEM, HBM],
        VMEM,
        [
            pltpu.VMEM((peers, chunks, CAP * LANE), BF16),
            pltpu.VMEM((CAP, peers * chunks, LANE), F32),
            pltpu.VMEM((slots, width), BF16),
            pltpu.SemaphoreType.DMA,
        ],
        16, 2 * slots * n * width, 2 << 20, "collect",
    )(ids, returned)
    return (token_grad, down_part.reshape(w_down.shape))


def solution(mesh):
    ranks = mesh.shape["dp"]
    split = Mesh(
        mesh.devices.reshape(mesh.shape["expert"], ranks // 2, 2), ("expert", "z", "core")
    )
    tokens = P(("expert", "z", "core"), None)
    experts = P("expert", None, None)
    features = P(("z", "core"), "expert", None)
    return jax.shard_map(
        on_device,
        mesh=split,
        in_specs=(tokens, tokens, tokens, tokens, experts, experts, features),
        out_specs=(tokens, features),
        check_vma=False,
    )
```

```python
import functools

import jax
import jax.numpy as jnp
from jax import lax
from jax.experimental import pallas as pl
from jax.experimental.pallas import tpu as pltpu
from jax.sharding import Mesh, PartitionSpec as P

CAP = 3
LANE = 128
NEAR = (0, -1, 1, -3, 3, -2, -4, 2)
BF16 = jnp.bfloat16
F32 = jnp.float32

VMEM = pl.BlockSpec(memory_space=pltpu.VMEM)
SMEM = pl.BlockSpec(memory_space=pltpu.SMEM)
HBM = pl.BlockSpec(memory_space=pltpu.HBM)


def mm(a, b, ca=1, cb=0):
    return lax.dot_general(a, b, (((ca,), (cb,)), ((), ())), preferred_element_type=F32)


def slots_of(ids_row, peers):
    n = ids_row.shape[1]
    across = jnp.broadcast_to(ids_row, (n, n))
    down = across.T
    row = lax.broadcasted_iota(jnp.int32, (n, n), 0)
    col = lax.broadcasted_iota(jnp.int32, (n, n), 1)
    earlier = jnp.where((across == down) & (row < col), 1.0, 0.0).astype(F32)
    rank = jnp.sum(earlier, axis=0, keepdims=True).astype(jnp.int32)
    return rank * peers + ids_row


def placing_of(ids_row, peers):
    n = ids_row.shape[1]
    lines = lax.broadcasted_iota(jnp.int32, (CAP * peers, n), 0)
    return jnp.where(lines == slots_of(ids_row, peers), 1.0, 0.0).astype(BF16)


def lanes(q, count=1):
    return slice(q * LANE, (q + count) * LANE)


def start_all(pairs, sems, base=0):
    copies = [
        pltpu.make_async_copy(source, target, sems.at[base + i])
        for i, (source, target) in enumerate(pairs)
    ]
    for copy in copies:
        copy.start()
    return copies


def pack_kernel(
    peers, ids_ref, weight_ref, tok_hbm, cot_hbm, own_hbm,
    out_hbm, passed_hbm,
    tok, cot, own, out, scr, sems,
):
    copies = start_all([(tok_hbm, tok), (cot_hbm, cot), (own_hbm, own)], sems)
    n, width = tok.shape
    chunks = width // LANE
    placing = placing_of(ids_ref[...], peers)
    weight = jnp.broadcast_to(weight_ref[...], (n, n)).T[:, :1]
    copies[2].wait()
    sent = start_all([(own, passed_hbm)], sems, 5)
    for which in range(2):
        copies[which].wait()
        for c in range(0, chunks, 2):
            if which == 0:
                rows = tok[:, lanes(c, 2)]
            else:
                rows = (weight * cot[:, lanes(c, 2)].astype(F32)).astype(BF16)
            placed = mm(placing, rows)
            for s in range(CAP):
                for h in range(2):
                    scr[CAP * which + s, pl.ds(c + h, peers, stride=chunks), :] = placed[
                        s * peers : (s + 1) * peers, lanes(h)
                    ]
        for q in range(CAP * which, CAP * which + CAP):
            out[which, :, :, lanes(q % CAP)] = (
                scr[q].reshape(peers, chunks, LANE).astype(BF16)
            )
        copy = pltpu.make_async_copy(
            out.at[which], out_hbm.at[:, :, pl.ds(which * CAP * LANE, CAP * LANE)], sems.at[3 + which]
        )
        copy.start()
        sent.append(copy)
    for copy in sent:
        copy.wait()


def to_rows(got, scr):
    peers, chunks, _ = got.shape
    for s in range(CAP):
        scr[s] = got[:, :, lanes(s)].astype(F32).reshape(peers * chunks, LANE)
    for s in range(CAP):
        for c in range(chunks):
            yield slice(s * peers, (s + 1) * peers), c, scr[s, pl.ds(c, peers, stride=chunks), :]


def forward_kernel(
    place_ref, got_hbm, wg_hbm, wu_hbm, after_hbm,
    send_hbm, keep_hbm, gate_hbm, up_hbm, cot_hbm,
    got, wg, wu, scr, rows, cot, own, other, gate, up, send, keep, sems,
):
    copies = start_all(
        [
            (got_hbm.at[:, :, pl.ds(0, CAP * LANE)], got.at[0]),
            (wg_hbm, wg),
            (wu_hbm, wu),
            (got_hbm.at[:, :, pl.ds(CAP * LANE, CAP * LANE)], got.at[1]),
        ],
        sems,
    )
    chunks = got.shape[2]
    first = place_ref[1] == 0
    copies[0].wait()
    for lines, c, value in to_rows(got.at[0], scr):
        rows[lines, lanes(c)] = value.astype(BF16)
    copies[1].wait()
    gate_value = mm(rows[...], wg[...])
    gate[...] = gate_value
    copies[2].wait()
    up_value = mm(rows[...], wu[...])
    up[...] = up_value
    hidden = (gate_value * jax.nn.sigmoid(gate_value) * up_value).astype(BF16)
    sent = start_all([(gate, gate_hbm), (up, up_hbm)], sems, 4)
    copies[3].wait()
    even = None
    for lines, c, value in to_rows(got.at[1], scr):
        cot[lines, lanes(c)] = value.astype(BF16)
        if c % 2 == 0:
            even = value
        else:
            own[lines, lanes(c // 2)] = jnp.where(first, even, value).astype(BF16)
            other[lines, lanes(c // 2)] = jnp.where(first, value, even).astype(BF16)
    sent += start_all([(cot, cot_hbm)], sems, 6)
    for i, (source, target, target_hbm) in enumerate(
        ((other, send, send_hbm), (own, keep, keep_hbm))
    ):
        for b in range(0, chunks // 2, 2):
            value = mm(source[:, lanes(b, 2)], hidden, 0, 0).astype(BF16)
            target[b] = value[:LANE]
            target[b + 1] = value[LANE:]
        sent += start_all([(target, target_hbm)], sems, 7 + i)
    for copy in sent:
        copy.wait()


def backward_kernel(
    place_ref, gate_hbm, up_hbm, cot_hbm,
    first_hbm, rest_hbm, first_other_hbm, rest_other_hbm, wg_hbm, wu_hbm,
    part_hbm,
    gate, up, cot, down, wg, wu, scr, part, sems,
):
    z, core = place_ref[0], place_ref[1]
    near = first_hbm.shape[0]
    chips = near + rest_hbm.shape[0]
    gathered = []
    for i, step in enumerate(NEAR):
        ahead = step * (1 - 2 * core)
        mine, theirs = (first_hbm, first_other_hbm) if i < near else (rest_hbm, rest_other_hbm)
        at = i if i < near else i - near
        chip = lax.rem(z + ahead + chips, chips)
        gathered.append((mine.at[at], down.at[chip * 2 + core]))
        chip = lax.rem(z - ahead + chips, chips)
        gathered.append((theirs.at[at], down.at[chip * 2 + 1 - core]))
    copies = start_all([(cot_hbm, cot)], sems)
    arriving = start_all(gathered, sems, 7)
    copies += start_all(
        [(gate_hbm, gate), (up_hbm, up), (wg_hbm, wg), (wu_hbm, wu)], sems, 1
    )
    peers, chunks, _ = part.shape
    copies[0].wait()
    for copy in arriving:
        copy.wait()
    grad = mm(cot[...], down[...].reshape(wg.shape))
    copies[1].wait()
    copies[2].wait()
    v = gate[...]
    sig = jax.nn.sigmoid(v)
    gate_grad = (grad * up[...] * sig * (1.0 + v * (1.0 - sig))).astype(BF16)
    up_grad = (grad * (v * sig)).astype(BF16)
    copies[3].wait()
    copies[4].wait()
    for c in range(0, chunks, 2):
        at = lanes(c, 2)
        value = mm(gate_grad, wg[at, :], 1, 1) + mm(up_grad, wu[at, :], 1, 1)
        for s in range(CAP):
            for h in range(2):
                scr[s, pl.ds(c + h, peers, stride=chunks), :] = value[
                    s * peers : (s + 1) * peers, lanes(h)
                ]
    for s in range(CAP):
        part[:, :, lanes(s)] = scr[s].reshape(peers, chunks, LANE).astype(BF16)
    for copy in start_all([(part, part_hbm)], sems, 5):
        copy.wait()


def fold_kernel(steps, place_ref, keep_hbm, swapped_hbm, *refs):
    targets, (kept, came, sems) = refs[: len(steps)], refs[len(steps) :]
    z, core = place_ref[0], place_ref[1]
    chips = keep_hbm.shape[0]
    copies = []
    for i, step in enumerate(steps):
        chip = lax.rem(z + step * (1 - 2 * core) + chips, chips)
        copies.append(
            start_all(
                [(keep_hbm.at[chip], kept.at[i]), (swapped_hbm.at[chip], came.at[i])], sems, 2 * i
            )
        )
    for i, target in enumerate(targets):
        for copy in copies[i]:
            copy.wait()
        target[...] = (kept[i].astype(F32) + came[i].astype(F32)).astype(target.dtype)


def collect_kernel(peers, ids_ref, got_hbm, out_ref, got, scr, rows, sem):
    copy = pltpu.make_async_copy(got_hbm, got, sem)
    copy.start()
    placing = placing_of(ids_ref[...], peers)
    copy.wait()
    for lines, c, value in to_rows(got, scr):
        rows[lines, lanes(c)] = value.astype(BF16)
    out_ref[...] = mm(placing, rows[...], 0, 0).astype(BF16)


def call(kernel, out_shape, in_specs, out_specs, scratch, limit, flops, moved, name):
    return pl.pallas_call(
        kernel,
        out_shape=out_shape,
        in_specs=in_specs,
        out_specs=out_specs,
        scratch_shapes=scratch,
        compiler_params=pltpu.CompilerParams(vmem_limit_bytes=limit << 20),
        cost_estimate=pl.CostEstimate(flops=flops, bytes_accessed=moved, transcendentals=0),
        name=name,
    )


def over_core(x):
    return lax.ppermute(x, "core", [(0, 1), (1, 0)])


def round_z(x, step):
    chips = lax.axis_size("z")
    pairs = [
        (2 * j + core, (j + step * (1 - 2 * core)) % chips * 2 + core)
        for j in range(chips)
        for core in range(2)
    ]
    return lax.ppermute(x, ("z", "core"), pairs)


def gather_features(own):
    m1, p1, m3, p3 = round_z(own, 1), round_z(own, -1), round_z(own, 3), round_z(own, -3)
    m2, m4 = jnp.split(round_z(jnp.concatenate([m1, m3]), 1), 2)
    p2 = round_z(p1, -1)
    first = jnp.stack([own, m1, p1, m3, p3])
    rest = jnp.stack([m2, m4, p2])
    return first, rest, over_core(first), over_core(rest)


def fold(steps, dtypes, place, keep, swapped):
    block = keep.shape[1:]
    count = len(steps)
    return call(
        functools.partial(fold_kernel, steps),
        tuple(jax.ShapeDtypeStruct(block, dtype) for dtype in dtypes),
        [SMEM, HBM, HBM],
        (VMEM,) * count,
        [
            pltpu.VMEM((count,) + block, BF16),
            pltpu.VMEM((count,) + block, BF16),
            pltpu.SemaphoreType.DMA((2 * count,)),
        ],
        24, keep.size, 6 * keep.size, "fold",
    )(place, keep, swapped)


def reduce_features(place, keep, swapped):
    below, above, above_far, far_below = fold((2, -2, -4, 3), (BF16,) * 4, place, keep, swapped)
    above = round_z(above, -1)
    above_far = round_z(above_far, -1)
    below = round_z(below, 1)
    far_below = round_z(far_below, 3)
    inner, outer, under, total = fold((-1, -3, 1, 0), (F32,) * 4, place, keep, swapped)
    far_above = round_z((outer + above_far.astype(F32)).astype(BF16), -3)
    near_above = round_z((inner + above.astype(F32)).astype(BF16), -1)
    near_below = round_z((under + below.astype(F32)).astype(BF16), 1)
    for arrived in (near_above, far_above, near_below, far_below):
        total = total + arrived.astype(F32)
    return total


def on_device(tokens, cotangent, expert_ids, route_weight, w_gate, w_up, w_down):
    n, width = tokens.shape
    peers = lax.axis_size("expert")
    ranks = lax.axis_size("z") * 2
    hidden = w_gate.shape[2]
    chunks = width // LANE
    slots = CAP * peers
    product = 2 * slots * width * hidden
    ids = expert_ids.reshape(1, n)
    weight = route_weight.reshape(1, n)
    wg = w_gate.reshape(width, hidden)
    wu = w_up.reshape(width, hidden)
    place = jnp.stack([lax.axis_index("z"), lax.axis_index("core")]).astype(jnp.int32)
    own = w_down.reshape(width // ranks, hidden)

    shape = jax.ShapeDtypeStruct
    packed, own = call(
        functools.partial(pack_kernel, peers),
        (shape((peers, chunks, 2 * CAP * LANE), BF16), shape(own.shape, BF16)),
        [VMEM, VMEM, HBM, HBM, HBM],
        (HBM, HBM),
        [
            pltpu.VMEM((n, width), BF16),
            pltpu.VMEM((n, width), BF16),
            pltpu.VMEM(own.shape, BF16),
            pltpu.VMEM((2, peers, chunks, CAP * LANE), BF16),
            pltpu.VMEM((2 * CAP, peers * chunks, LANE), F32),
            pltpu.SemaphoreType.DMA((6,)),
        ],
        58, 4 * slots * n * width, 4 << 20, "pack",
    )(ids, weight, tokens, cotangent, own)
    got = lax.all_to_all(packed, "expert", split_axis=0, concat_axis=0, tiled=True)
    gathered = gather_features(own)

    weights = pltpu.VMEM((width, hidden), BF16)
    features = pltpu.VMEM((chunks // 2, LANE, hidden), BF16)
    inner = pltpu.VMEM((slots, hidden), F32)
    send, keep, gate, up, cot = call(
        forward_kernel,
        (
            shape((chunks // 2, LANE, hidden), BF16),
            shape((chunks // 2, LANE, hidden), BF16),
            shape((slots, hidden), F32),
            shape((slots, hidden), F32),
            shape((slots, width), BF16),
        ),
        [SMEM] + [HBM] * 4,
        (HBM,) * 5,
        [
            pltpu.VMEM((2, peers, chunks, CAP * LANE), BF16),
            weights,
            weights,
            pltpu.VMEM((CAP, peers * chunks, LANE), F32),
            pltpu.VMEM((slots, width), BF16),
            pltpu.VMEM((slots, width), BF16),
            pltpu.VMEM((slots, width // 2), BF16),
            pltpu.VMEM((slots, width // 2), BF16),
            inner,
            inner,
            features,
            features,
            pltpu.SemaphoreType.DMA((9,)),
        ],
        62, 3 * product, 14 << 20, "forward",
    )(place, got, wg, wu, gathered[1])
    swapped = over_core(send)

    part = call(
        backward_kernel,
        shape((peers, chunks, CAP * LANE), BF16),
        [SMEM] + [HBM] * 9,
        HBM,
        [
            inner,
            inner,
            pltpu.VMEM((slots, width), BF16),
            pltpu.VMEM((chunks, LANE, hidden), BF16),
            weights,
            weights,
            pltpu.VMEM((CAP, peers * chunks, LANE), F32),
            pltpu.VMEM((peers, chunks, CAP * LANE), BF16),
            pltpu.SemaphoreType.DMA((7 + chunks,)),
        ],
        62, 3 * product, 14 << 20, "backward",
    )(place, gate, up, cot, *gathered, wg, wu)

    down_part = reduce_features(place, keep, swapped)
    returned = lax.all_to_all(part, "expert", split_axis=0, concat_axis=0, tiled=True)

    token_grad = call(
        functools.partial(collect_kernel, peers),
        shape((n, width), BF16),
        [VMEM, HBM],
        VMEM,
        [
            pltpu.VMEM((peers, chunks, CAP * LANE), BF16),
            pltpu.VMEM((CAP, peers * chunks, LANE), F32),
            pltpu.VMEM((slots, width), BF16),
            pltpu.SemaphoreType.DMA,
        ],
        16, 2 * slots * n * width, 2 << 20, "collect",
    )(ids, returned)
    return (token_grad, down_part.reshape(w_down.shape))


def solution(mesh):
    ranks = mesh.shape["dp"]
    split = Mesh(
        mesh.devices.reshape(mesh.shape["expert"], ranks // 2, 2), ("expert", "z", "core")
    )
    tokens = P(("expert", "z", "core"), None)
    experts = P("expert", None, None)
    features = P(("z", "core"), "expert", None)
    return jax.shard_map(
        on_device,
        mesh=split,
        in_specs=(tokens, tokens, tokens, tokens, experts, experts, features),
        out_specs=(tokens, features),
        check_vma=False,
    )
```

```python
import functools

import jax
import jax.numpy as jnp
from jax import lax
from jax.experimental import pallas as pl
from jax.experimental.pallas import tpu as pltpu
from jax.sharding import Mesh, PartitionSpec as P

CAP = 3
LANE = 128
NEAR = (0, -1, 1, -3, 3, -2, -4, 2)
FOLD = (-2, -4, 2, 3, -3, -1, 1, 0)
BF16 = jnp.bfloat16
F32 = jnp.float32

VMEM = pl.BlockSpec(memory_space=pltpu.VMEM)
SMEM = pl.BlockSpec(memory_space=pltpu.SMEM)
HBM = pl.BlockSpec(memory_space=pltpu.HBM)


def mm(a, b, ca=1, cb=0):
    return lax.dot_general(a, b, (((ca,), (cb,)), ((), ())), preferred_element_type=F32)


def slots_of(ids_row, peers):
    n = ids_row.shape[1]
    across = jnp.broadcast_to(ids_row, (n, n))
    down = across.T
    row = lax.broadcasted_iota(jnp.int32, (n, n), 0)
    col = lax.broadcasted_iota(jnp.int32, (n, n), 1)
    earlier = jnp.where((across == down) & (row < col), 1.0, 0.0).astype(F32)
    rank = jnp.sum(earlier, axis=0, keepdims=True).astype(jnp.int32)
    return rank * peers + ids_row


def placing_of(ids_row, peers):
    n = ids_row.shape[1]
    lines = lax.broadcasted_iota(jnp.int32, (CAP * peers, n), 0)
    return jnp.where(lines == slots_of(ids_row, peers), 1.0, 0.0).astype(BF16)


def lanes(q, count=1):
    return slice(q * LANE, (q + count) * LANE)


def start_all(pairs, sems, base=0):
    copies = [
        pltpu.make_async_copy(source, target, sems.at[base + i])
        for i, (source, target) in enumerate(pairs)
    ]
    for copy in copies:
        copy.start()
    return copies


def pack_kernel(
    peers, ids_ref, weight_ref, tok_hbm, cot_hbm, own_hbm,
    out_hbm, passed_hbm,
    tok, cot, own, out, scr, sems,
):
    copies = start_all([(tok_hbm, tok), (cot_hbm, cot), (own_hbm, own)], sems)
    n, width = tok.shape
    chunks = width // LANE
    placing = placing_of(ids_ref[...], peers)
    weight = jnp.broadcast_to(weight_ref[...], (n, n)).T[:, :1]
    copies[2].wait()
    sent = start_all([(own, passed_hbm)], sems, 5)
    for which in range(2):
        copies[which].wait()
        for c in range(0, chunks, 2):
            if which == 0:
                rows = tok[:, lanes(c, 2)]
            else:
                rows = (weight * cot[:, lanes(c, 2)].astype(F32)).astype(BF16)
            placed = mm(placing, rows)
            for s in range(CAP):
                for h in range(2):
                    scr[CAP * which + s, pl.ds(c + h, peers, stride=chunks), :] = placed[
                        s * peers : (s + 1) * peers, lanes(h)
                    ]
        for q in range(CAP * which, CAP * which + CAP):
            out[which, :, :, lanes(q % CAP)] = (
                scr[q].reshape(peers, chunks, LANE).astype(BF16)
            )
        copy = pltpu.make_async_copy(
            out.at[which], out_hbm.at[:, :, pl.ds(which * CAP * LANE, CAP * LANE)], sems.at[3 + which]
        )
        copy.start()
        sent.append(copy)
    for copy in sent:
        copy.wait()


def to_rows(got, scr):
    peers, chunks, _ = got.shape
    for s in range(CAP):
        scr[s] = got[:, :, lanes(s)].astype(F32).reshape(peers * chunks, LANE)
    for s in range(CAP):
        for c in range(chunks):
            yield slice(s * peers, (s + 1) * peers), c, scr[s, pl.ds(c, peers, stride=chunks), :]


def forward_kernel(
    place_ref, got_hbm, wg_hbm, wu_hbm, after_hbm,
    send_a_hbm, send_b_hbm, keep_a_hbm, keep_b_hbm, gate_hbm, up_hbm, cot_hbm,
    got, wg, wu, scr, rows, cot, own, other, gate, up, send, keep, sems,
):
    copies = start_all(
        [
            (got_hbm.at[:, :, pl.ds(0, CAP * LANE)], got.at[0]),
            (wg_hbm, wg),
            (wu_hbm, wu),
            (got_hbm.at[:, :, pl.ds(CAP * LANE, CAP * LANE)], got.at[1]),
        ],
        sems,
    )
    chunks = got.shape[2]
    z, core = place_ref[0], place_ref[1]
    first = core == 0
    copies[0].wait()
    for lines, c, value in to_rows(got.at[0], scr):
        rows[lines, lanes(c)] = value.astype(BF16)
    copies[1].wait()
    gate_value = mm(rows[...], wg[...])
    gate[...] = gate_value
    copies[2].wait()
    up_value = mm(rows[...], wu[...])
    up[...] = up_value
    hidden = (gate_value * jax.nn.sigmoid(gate_value) * up_value).astype(BF16)
    sent = start_all([(gate, gate_hbm), (up, up_hbm)], sems, 4)
    copies[3].wait()
    even = None
    for lines, c, value in to_rows(got.at[1], scr):
        cot[lines, lanes(c)] = value.astype(BF16)
        if c % 2 == 0:
            even = value
        else:
            own[lines, lanes(c // 2)] = jnp.where(first, even, value).astype(BF16)
            other[lines, lanes(c // 2)] = jnp.where(first, value, even).astype(BF16)
    sent += start_all([(cot, cot_hbm)], sems, 6)
    chips = chunks // 2
    half = chips // 2
    for i, (source, target, a_hbm, b_hbm, ahead) in enumerate(
        (
            (other, send, send_a_hbm, send_b_hbm, 2 * core - 1),
            (own, keep, keep_a_hbm, keep_b_hbm, 1 - 2 * core),
        )
    ):
        for b in range(0, chips, 2):
            value = mm(source[:, lanes(b, 2)], hidden, 0, 0).astype(BF16)
            target[b] = value[:LANE]
            target[b + 1] = value[LANE:]
        moves = []
        for at, step in enumerate(FOLD):
            chip = lax.rem(z + step * ahead + chips, chips)
            moves.append((target.at[chip], (a_hbm if at < half else b_hbm).at[at % half]))
        sent += start_all(moves, sems, 7 + i * chips)
    for copy in sent:
        copy.wait()


def backward_kernel(
    place_ref, gate_hbm, up_hbm, cot_hbm,
    first_hbm, rest_hbm, first_other_hbm, rest_other_hbm, wg_hbm, wu_hbm, after_hbm,
    part_hbm,
    gate, up, cot, down, wg, wu, scr, part, sems,
):
    z, core = place_ref[0], place_ref[1]
    near = first_hbm.shape[0]
    chips = near + rest_hbm.shape[0]
    gathered = []
    for i, step in enumerate(NEAR):
        ahead = step * (1 - 2 * core)
        mine, theirs = (first_hbm, first_other_hbm) if i < near else (rest_hbm, rest_other_hbm)
        at = i if i < near else i - near
        chip = lax.rem(z + ahead + chips, chips)
        gathered.append((mine.at[at], down.at[chip * 2 + core]))
        chip = lax.rem(z - ahead + chips, chips)
        gathered.append((theirs.at[at], down.at[chip * 2 + 1 - core]))
    copies = start_all([(cot_hbm, cot)], sems)
    arriving = start_all(gathered, sems, 7)
    copies += start_all(
        [(gate_hbm, gate), (up_hbm, up), (wg_hbm, wg), (wu_hbm, wu)], sems, 1
    )
    peers, chunks, _ = part.shape
    copies[0].wait()
    for copy in arriving:
        copy.wait()
    grad = mm(cot[...], down[...].reshape(wg.shape))
    copies[1].wait()
    copies[2].wait()
    v = gate[...]
    sig = jax.nn.sigmoid(v)
    gate_grad = (grad * up[...] * sig * (1.0 + v * (1.0 - sig))).astype(BF16)
    up_grad = (grad * (v * sig)).astype(BF16)
    copies[3].wait()
    copies[4].wait()
    for c in range(0, chunks, 2):
        at = lanes(c, 2)
        value = mm(gate_grad, wg[at, :], 1, 1) + mm(up_grad, wu[at, :], 1, 1)
        for s in range(CAP):
            for h in range(2):
                scr[s, pl.ds(c + h, peers, stride=chunks), :] = value[
                    s * peers : (s + 1) * peers, lanes(h)
                ]
    for s in range(CAP):
        part[:, :, lanes(s)] = scr[s].reshape(peers, chunks, LANE).astype(BF16)
    for copy in start_all([(part, part_hbm)], sems, 5):
        copy.wait()


def collect_kernel(peers, ids_ref, got_hbm, out_ref, got, scr, rows, sem):
    copy = pltpu.make_async_copy(got_hbm, got, sem)
    copy.start()
    placing = placing_of(ids_ref[...], peers)
    copy.wait()
    for lines, c, value in to_rows(got, scr):
        rows[lines, lanes(c)] = value.astype(BF16)
    out_ref[...] = mm(placing, rows[...], 0, 0).astype(BF16)


def call(kernel, out_shape, in_specs, out_specs, scratch, limit, flops, moved, name):
    return pl.pallas_call(
        kernel,
        out_shape=out_shape,
        in_specs=in_specs,
        out_specs=out_specs,
        scratch_shapes=scratch,
        compiler_params=pltpu.CompilerParams(vmem_limit_bytes=limit << 20),
        cost_estimate=pl.CostEstimate(flops=flops, bytes_accessed=moved, transcendentals=0),
        name=name,
    )


def over_core(x):
    return lax.ppermute(x, "core", [(0, 1), (1, 0)])


def round_z(x, step):
    chips = lax.axis_size("z")
    pairs = [
        (2 * j + core, (j + step * (1 - 2 * core)) % chips * 2 + core)
        for j in range(chips)
        for core in range(2)
    ]
    return lax.ppermute(x, ("z", "core"), pairs)


def gather_features(own):
    m1, p1, m3, p3 = round_z(own, 1), round_z(own, -1), round_z(own, 3), round_z(own, -3)
    m2, m4 = jnp.split(round_z(jnp.concatenate([m1, m3]), 1), 2)
    p2 = round_z(p1, -1)
    first = jnp.stack([own, m1, p1, m3, p3])
    rest = jnp.stack([m2, m4, p2])
    return first, rest, over_core(first), over_core(rest)


def reduce_features(above, below, far_below, keep, swapped):
    outer, inner, under, total = [
        keep[i].astype(F32) + swapped[i].astype(F32) for i in range(keep.shape[0])
    ]
    far_above = round_z((outer + above[1].astype(F32)).astype(BF16), -3)
    near_above = round_z((inner + above[0].astype(F32)).astype(BF16), -1)
    near_below = round_z((under + below.astype(F32)).astype(BF16), 1)
    for arrived in (near_above, far_above, near_below, far_below):
        total = total + arrived.astype(F32)
    return total


def on_device(tokens, cotangent, expert_ids, route_weight, w_gate, w_up, w_down):
    n, width = tokens.shape
    peers = lax.axis_size("expert")
    ranks = lax.axis_size("z") * 2
    hidden = w_gate.shape[2]
    chunks = width // LANE
    slots = CAP * peers
    product = 2 * slots * width * hidden
    ids = expert_ids.reshape(1, n)
    weight = route_weight.reshape(1, n)
    wg = w_gate.reshape(width, hidden)
    wu = w_up.reshape(width, hidden)
    place = jnp.stack([lax.axis_index("z"), lax.axis_index("core")]).astype(jnp.int32)
    own = w_down.reshape(width // ranks, hidden)

    shape = jax.ShapeDtypeStruct
    packed, own = call(
        functools.partial(pack_kernel, peers),
        (shape((peers, chunks, 2 * CAP * LANE), BF16), shape(own.shape, BF16)),
        [VMEM, VMEM, HBM, HBM, HBM],
        (HBM, HBM),
        [
            pltpu.VMEM((n, width), BF16),
            pltpu.VMEM((n, width), BF16),
            pltpu.VMEM(own.shape, BF16),
            pltpu.VMEM((2, peers, chunks, CAP * LANE), BF16),
            pltpu.VMEM((2 * CAP, peers * chunks, LANE), F32),
            pltpu.SemaphoreType.DMA((6,)),
        ],
        58, 4 * slots * n * width, 4 << 20, "pack",
    )(ids, weight, tokens, cotangent, own)
    got = lax.all_to_all(packed, "expert", split_axis=0, concat_axis=0, tiled=True)
    gathered = gather_features(own)

    weights = pltpu.VMEM((width, hidden), BF16)
    features = pltpu.VMEM((chunks // 2, LANE, hidden), BF16)
    inner = pltpu.VMEM((slots, hidden), F32)
    quarter = shape((chunks // 4, LANE, hidden), BF16)
    send_a, send_b, keep_a, keep_b, gate, up, cot = call(
        forward_kernel,
        (
            quarter,
            quarter,
            quarter,
            quarter,
            shape((slots, hidden), F32),
            shape((slots, hidden), F32),
            shape((slots, width), BF16),
        ),
        [SMEM] + [HBM] * 4,
        (HBM,) * 7,
        [
            pltpu.VMEM((2, peers, chunks, CAP * LANE), BF16),
            weights,
            weights,
            pltpu.VMEM((CAP, peers * chunks, LANE), F32),
            pltpu.VMEM((slots, width), BF16),
            pltpu.VMEM((slots, width), BF16),
            pltpu.VMEM((slots, width // 2), BF16),
            pltpu.VMEM((slots, width // 2), BF16),
            inner,
            inner,
            features,
            features,
            pltpu.SemaphoreType.DMA((7 + chunks,)),
        ],
        62, 3 * product, 14 << 20, "forward",
    )(place, got, wg, wu, gathered[1])
    swapped_a = over_core(send_a)
    swapped_b = over_core(send_b)
    outward = (keep_a.astype(F32) + swapped_a.astype(F32)).astype(BF16)
    above = round_z(outward[:2], -1)
    below = round_z(outward[2], 1)
    far_below = round_z(outward[3], 3)

    part = call(
        backward_kernel,
        shape((peers, chunks, CAP * LANE), BF16),
        [SMEM] + [HBM] * 10,
        HBM,
        [
            inner,
            inner,
            pltpu.VMEM((slots, width), BF16),
            pltpu.VMEM((chunks, LANE, hidden), BF16),
            weights,
            weights,
            pltpu.VMEM((CAP, peers * chunks, LANE), F32),
            pltpu.VMEM((peers, chunks, CAP * LANE), BF16),
            pltpu.SemaphoreType.DMA((7 + chunks,)),
        ],
        62, 3 * product, 14 << 20, "backward",
    )(place, gate, up, cot, *gathered, wg, wu, above)

    down_part = reduce_features(above, below, far_below, keep_b, swapped_b)
    returned = lax.all_to_all(part, "expert", split_axis=0, concat_axis=0, tiled=True)

    token_grad = call(
        functools.partial(collect_kernel, peers),
        shape((n, width), BF16),
        [VMEM, HBM],
        VMEM,
        [
            pltpu.VMEM((peers, chunks, CAP * LANE), BF16),
            pltpu.VMEM((CAP, peers * chunks, LANE), F32),
            pltpu.VMEM((slots, width), BF16),
            pltpu.SemaphoreType.DMA,
        ],
        16, 2 * slots * n * width, 2 << 20, "collect",
    )(ids, returned)
    return (token_grad, down_part.reshape(w_down.shape))


def solution(mesh):
    ranks = mesh.shape["dp"]
    split = Mesh(
        mesh.devices.reshape(mesh.shape["expert"], ranks // 2, 2), ("expert", "z", "core")
    )
    tokens = P(("expert", "z", "core"), None)
    experts = P("expert", None, None)
    features = P(("z", "core"), "expert", None)
    return jax.shard_map(
        on_device,
        mesh=split,
        in_specs=(tokens, tokens, tokens, tokens, experts, experts, features),
        out_specs=(tokens, features),
        check_vma=False,
    )
```

```python
import functools

import jax
import jax.numpy as jnp
from jax import lax
from jax.experimental import pallas as pl
from jax.experimental.pallas import tpu as pltpu
from jax.sharding import Mesh, PartitionSpec as P

CAP = 3
LANE = 128
NEAR = (0, -1, 1, -3, 3, -2, -4, 2)
FOLD = (-2, -4, 2, 3, -3, -1, 1, 0)
BF16 = jnp.bfloat16
F32 = jnp.float32

VMEM = pl.BlockSpec(memory_space=pltpu.VMEM)
SMEM = pl.BlockSpec(memory_space=pltpu.SMEM)
HBM = pl.BlockSpec(memory_space=pltpu.HBM)


def mm(a, b, ca=1, cb=0):
    return lax.dot_general(a, b, (((ca,), (cb,)), ((), ())), preferred_element_type=F32)


def slots_of(ids_row, peers):
    n = ids_row.shape[1]
    across = jnp.broadcast_to(ids_row, (n, n))
    down = across.T
    row = lax.broadcasted_iota(jnp.int32, (n, n), 0)
    col = lax.broadcasted_iota(jnp.int32, (n, n), 1)
    earlier = jnp.where((across == down) & (row < col), 1.0, 0.0).astype(F32)
    rank = jnp.sum(earlier, axis=0, keepdims=True).astype(jnp.int32)
    return rank * peers + ids_row


def placing_of(ids_row, peers):
    n = ids_row.shape[1]
    lines = lax.broadcasted_iota(jnp.int32, (CAP * peers, n), 0)
    return jnp.where(lines == slots_of(ids_row, peers), 1.0, 0.0).astype(BF16)


def lanes(q, count=1):
    return slice(q * LANE, (q + count) * LANE)


def start_all(pairs, sems, base=0):
    copies = [
        pltpu.make_async_copy(source, target, sems.at[base + i])
        for i, (source, target) in enumerate(pairs)
    ]
    for copy in copies:
        copy.start()
    return copies


def pack_kernel(
    peers, ids_ref, weight_ref, tok_hbm, cot_hbm, own_hbm,
    out_hbm, passed_hbm,
    tok, cot, own, out, scr, sems,
):
    copies = start_all([(tok_hbm, tok), (cot_hbm, cot), (own_hbm, own)], sems)
    n, width = tok.shape
    chunks = width // LANE
    placing = placing_of(ids_ref[...], peers)
    weight = jnp.broadcast_to(weight_ref[...], (n, n)).T[:, :1]
    copies[2].wait()
    sent = start_all([(own, passed_hbm)], sems, 5)
    for which in range(2):
        copies[which].wait()
        for c in range(0, chunks, 2):
            if which == 0:
                rows = tok[:, lanes(c, 2)]
            else:
                rows = (weight * cot[:, lanes(c, 2)].astype(F32)).astype(BF16)
            placed = mm(placing, rows)
            for s in range(CAP):
                for h in range(2):
                    scr[CAP * which + s, pl.ds(c + h, peers, stride=chunks), :] = placed[
                        s * peers : (s + 1) * peers, lanes(h)
                    ]
        for q in range(CAP * which, CAP * which + CAP):
            out[which, :, :, lanes(q % CAP)] = (
                scr[q].reshape(peers, chunks, LANE).astype(BF16)
            )
        copy = pltpu.make_async_copy(
            out.at[which], out_hbm.at[:, :, pl.ds(which * CAP * LANE, CAP * LANE)], sems.at[3 + which]
        )
        copy.start()
        sent.append(copy)
    for copy in sent:
        copy.wait()


def to_rows(got, scr):
    peers, chunks, _ = got.shape
    for s in range(CAP):
        scr[s] = got[:, :, lanes(s)].astype(F32).reshape(peers * chunks, LANE)
    for s in range(CAP):
        for c in range(chunks):
            yield slice(s * peers, (s + 1) * peers), c, scr[s, pl.ds(c, peers, stride=chunks), :]


def forward_kernel(
    place_ref, got_hbm, wg_hbm, wu_hbm, after_hbm,
    send_a_hbm, send_b_hbm, keep_a_hbm, keep_b_hbm, gate_hbm, up_hbm, cot_hbm,
    got, wg, wu, scr, rows, cot, own, other, gate, up, send, keep, sems,
):
    copies = start_all(
        [
            (got_hbm.at[:, :, pl.ds(0, CAP * LANE)], got.at[0]),
            (wg_hbm, wg),
            (wu_hbm, wu),
            (got_hbm.at[:, :, pl.ds(CAP * LANE, CAP * LANE)], got.at[1]),
        ],
        sems,
    )
    chunks = got.shape[2]
    z, core = place_ref[0], place_ref[1]
    first = core == 0
    copies[0].wait()
    for lines, c, value in to_rows(got.at[0], scr):
        rows[lines, lanes(c)] = value.astype(BF16)
    copies[1].wait()
    gate_value = mm(rows[...], wg[...])
    gate[...] = gate_value
    copies[2].wait()
    up_value = mm(rows[...], wu[...])
    up[...] = up_value
    hidden = (gate_value * jax.nn.sigmoid(gate_value) * up_value).astype(BF16)
    sent = start_all([(gate, gate_hbm), (up, up_hbm)], sems, 4)
    copies[3].wait()
    even = None
    for lines, c, value in to_rows(got.at[1], scr):
        cot[lines, lanes(c)] = value.astype(BF16)
        if c % 2 == 0:
            even = value
        else:
            own[lines, lanes(c // 2)] = jnp.where(first, even, value).astype(BF16)
            other[lines, lanes(c // 2)] = jnp.where(first, value, even).astype(BF16)
    sent += start_all([(cot, cot_hbm)], sems, 6)
    chips = chunks // 2
    half = chips // 2
    for i, (source, target, a_hbm, b_hbm, ahead) in enumerate(
        (
            (other, send, send_a_hbm, send_b_hbm, 2 * core - 1),
            (own, keep, keep_a_hbm, keep_b_hbm, 1 - 2 * core),
        )
    ):
        for b in range(0, chips, 2):
            value = mm(source[:, lanes(b, 2)], hidden, 0, 0).astype(BF16)
            target[b] = value[:LANE]
            target[b + 1] = value[LANE:]
        moves = []
        for at, step in enumerate(FOLD):
            chip = lax.rem(z + step * ahead + chips, chips)
            moves.append((target.at[chip], (a_hbm if at < half else b_hbm).at[at % half]))
        sent += start_all(moves, sems, 7 + i * chips)
    for copy in sent:
        copy.wait()


def backward_kernel(
    place_ref, gate_hbm, up_hbm, cot_hbm,
    first_hbm, rest_hbm, first_other_hbm, rest_other_hbm, wg_hbm, wu_hbm,
    part_hbm,
    gate, up, cot, down, wg, wu, scr, part, sems,
):
    z, core = place_ref[0], place_ref[1]
    near = first_hbm.shape[0]
    chips = near + rest_hbm.shape[0]
    gathered = []
    for i, step in enumerate(NEAR):
        ahead = step * (1 - 2 * core)
        mine, theirs = (first_hbm, first_other_hbm) if i < near else (rest_hbm, rest_other_hbm)
        at = i if i < near else i - near
        chip = lax.rem(z + ahead + chips, chips)
        gathered.append((mine.at[at], down.at[chip * 2 + core]))
        chip = lax.rem(z - ahead + chips, chips)
        gathered.append((theirs.at[at], down.at[chip * 2 + 1 - core]))
    copies = start_all([(cot_hbm, cot)], sems)
    arriving = start_all(gathered, sems, 7)
    copies += start_all(
        [(gate_hbm, gate), (up_hbm, up), (wg_hbm, wg), (wu_hbm, wu)], sems, 1
    )
    peers, chunks, _ = part.shape
    copies[0].wait()
    for copy in arriving:
        copy.wait()
    grad = mm(cot[...], down[...].reshape(wg.shape))
    copies[1].wait()
    copies[2].wait()
    v = gate[...]
    sig = jax.nn.sigmoid(v)
    gate_grad = (grad * up[...] * sig * (1.0 + v * (1.0 - sig))).astype(BF16)
    up_grad = (grad * (v * sig)).astype(BF16)
    copies[3].wait()
    copies[4].wait()
    for c in range(0, chunks, 2):
        at = lanes(c, 2)
        value = mm(gate_grad, wg[at, :], 1, 1) + mm(up_grad, wu[at, :], 1, 1)
        for s in range(CAP):
            for h in range(2):
                scr[s, pl.ds(c + h, peers, stride=chunks), :] = value[
                    s * peers : (s + 1) * peers, lanes(h)
                ]
    for s in range(CAP):
        part[:, :, lanes(s)] = scr[s].reshape(peers, chunks, LANE).astype(BF16)
    for copy in start_all([(part, part_hbm)], sems, 5):
        copy.wait()


def collect_kernel(peers, ids_ref, got_hbm, out_ref, got, scr, rows, sem):
    copy = pltpu.make_async_copy(got_hbm, got, sem)
    copy.start()
    placing = placing_of(ids_ref[...], peers)
    copy.wait()
    for lines, c, value in to_rows(got, scr):
        rows[lines, lanes(c)] = value.astype(BF16)
    out_ref[...] = mm(placing, rows[...], 0, 0).astype(BF16)


def call(kernel, out_shape, in_specs, out_specs, scratch, limit, flops, moved, name):
    return pl.pallas_call(
        kernel,
        out_shape=out_shape,
        in_specs=in_specs,
        out_specs=out_specs,
        scratch_shapes=scratch,
        compiler_params=pltpu.CompilerParams(vmem_limit_bytes=limit << 20),
        cost_estimate=pl.CostEstimate(flops=flops, bytes_accessed=moved, transcendentals=0),
        name=name,
    )


def over_core(x):
    return lax.ppermute(x, "core", [(0, 1), (1, 0)])


def round_z(x, step):
    chips = lax.axis_size("z")
    pairs = [
        (2 * j + core, (j + step * (1 - 2 * core)) % chips * 2 + core)
        for j in range(chips)
        for core in range(2)
    ]
    return lax.ppermute(x, ("z", "core"), pairs)


def gather_features(own):
    m1, p1, m3, p3 = round_z(own, 1), round_z(own, -1), round_z(own, 3), round_z(own, -3)
    m2, m4 = jnp.split(round_z(jnp.concatenate([m1, m3]), 1), 2)
    p2 = round_z(p1, -1)
    first = jnp.stack([own, m1, p1, m3, p3])
    rest = jnp.stack([m2, m4, p2])
    return first, rest, over_core(first), over_core(rest)


def reduce_features(above, below, far_below, keep, swapped):
    outer, inner, under, total = [
        keep[i].astype(F32) + swapped[i].astype(F32) for i in range(keep.shape[0])
    ]
    far_above = round_z((outer + above[1].astype(F32)).astype(BF16), -3)
    near_above = round_z((inner + above[0].astype(F32)).astype(BF16), -1)
    near_below = round_z((under + below.astype(F32)).astype(BF16), 1)
    for arrived in (near_above, far_above, near_below, far_below):
        total = total + arrived.astype(F32)
    return total


def on_device(tokens, cotangent, expert_ids, route_weight, w_gate, w_up, w_down):
    n, width = tokens.shape
    peers = lax.axis_size("expert")
    ranks = lax.axis_size("z") * 2
    hidden = w_gate.shape[2]
    chunks = width // LANE
    slots = CAP * peers
    product = 2 * slots * width * hidden
    ids = expert_ids.reshape(1, n)
    weight = route_weight.reshape(1, n)
    wg = w_gate.reshape(width, hidden)
    wu = w_up.reshape(width, hidden)
    place = jnp.stack([lax.axis_index("z"), lax.axis_index("core")]).astype(jnp.int32)
    own = w_down.reshape(width // ranks, hidden)

    shape = jax.ShapeDtypeStruct
    packed, own = call(
        functools.partial(pack_kernel, peers),
        (shape((peers, chunks, 2 * CAP * LANE), BF16), shape(own.shape, BF16)),
        [VMEM, VMEM, HBM, HBM, HBM],
        (HBM, HBM),
        [
            pltpu.VMEM((n, width), BF16),
            pltpu.VMEM((n, width), BF16),
            pltpu.VMEM(own.shape, BF16),
            pltpu.VMEM((2, peers, chunks, CAP * LANE), BF16),
            pltpu.VMEM((2 * CAP, peers * chunks, LANE), F32),
            pltpu.SemaphoreType.DMA((6,)),
        ],
        58, 4 * slots * n * width, 4 << 20, "pack",
    )(ids, weight, tokens, cotangent, own)
    got = lax.all_to_all(packed, "expert", split_axis=0, concat_axis=0, tiled=True)
    gathered = gather_features(own)

    weights = pltpu.VMEM((width, hidden), BF16)
    features = pltpu.VMEM((chunks // 2, LANE, hidden), BF16)
    inner = pltpu.VMEM((slots, hidden), F32)
    quarter = shape((chunks // 4, LANE, hidden), BF16)
    send_a, send_b, keep_a, keep_b, gate, up, cot = call(
        forward_kernel,
        (
            quarter,
            quarter,
            quarter,
            quarter,
            shape((slots, hidden), F32),
            shape((slots, hidden), F32),
            shape((slots, width), BF16),
        ),
        [SMEM] + [HBM] * 4,
        (HBM,) * 7,
        [
            pltpu.VMEM((2, peers, chunks, CAP * LANE), BF16),
            weights,
            weights,
            pltpu.VMEM((CAP, peers * chunks, LANE), F32),
            pltpu.VMEM((slots, width), BF16),
            pltpu.VMEM((slots, width), BF16),
            pltpu.VMEM((slots, width // 2), BF16),
            pltpu.VMEM((slots, width // 2), BF16),
            inner,
            inner,
            features,
            features,
            pltpu.SemaphoreType.DMA((7 + chunks,)),
        ],
        62, 3 * product, 14 << 20, "forward",
    )(place, got, wg, wu, gathered[1])
    swapped_a = over_core(send_a)
    swapped_b = over_core(send_b)
    outward = (keep_a.astype(F32) + swapped_a.astype(F32)).astype(BF16)
    above = round_z(outward[:2], -1)
    below = round_z(outward[2], 1)
    far_below = round_z(outward[3], 3)

    part = call(
        backward_kernel,
        shape((peers, chunks, CAP * LANE), BF16),
        [SMEM] + [HBM] * 9,
        HBM,
        [
            inner,
            inner,
            pltpu.VMEM((slots, width), BF16),
            pltpu.VMEM((chunks, LANE, hidden), BF16),
            weights,
            weights,
            pltpu.VMEM((CAP, peers * chunks, LANE), F32),
            pltpu.VMEM((peers, chunks, CAP * LANE), BF16),
            pltpu.SemaphoreType.DMA((7 + chunks,)),
        ],
        62, 3 * product, 14 << 20, "backward",
    )(place, gate, up, cot, *gathered, wg, wu)

    down_part = reduce_features(above, below, far_below, keep_b, swapped_b)
    returned = lax.all_to_all(part, "expert", split_axis=0, concat_axis=0, tiled=True)

    token_grad = call(
        functools.partial(collect_kernel, peers),
        shape((n, width), BF16),
        [VMEM, HBM],
        VMEM,
        [
            pltpu.VMEM((peers, chunks, CAP * LANE), BF16),
            pltpu.VMEM((CAP, peers * chunks, LANE), F32),
            pltpu.VMEM((slots, width), BF16),
            pltpu.SemaphoreType.DMA,
        ],
        16, 2 * slots * n * width, 2 << 20, "collect",
    )(ids, returned)
    return (token_grad, down_part.reshape(w_down.shape))


def solution(mesh):
    ranks = mesh.shape["dp"]
    split = Mesh(
        mesh.devices.reshape(mesh.shape["expert"], ranks // 2, 2), ("expert", "z", "core")
    )
    tokens = P(("expert", "z", "core"), None)
    experts = P("expert", None, None)
    features = P(("z", "core"), "expert", None)
    return jax.shard_map(
        on_device,
        mesh=split,
        in_specs=(tokens, tokens, tokens, tokens, experts, experts, features),
        out_specs=(tokens, features),
        check_vma=False,
    )
```

```python
import functools

import jax
import jax.numpy as jnp
from jax import lax
from jax.experimental import pallas as pl
from jax.experimental.pallas import tpu as pltpu
from jax.sharding import Mesh, PartitionSpec as P

CAP = 3
LANE = 128
NEAR = (0, -1, 1, -3, 3, -2, -4, 2)
FOLD = (-2, -4, 2, 3, -3, -1, 1, 0)
BF16 = jnp.bfloat16
F32 = jnp.float32

VMEM = pl.BlockSpec(memory_space=pltpu.VMEM)
SMEM = pl.BlockSpec(memory_space=pltpu.SMEM)
HBM = pl.BlockSpec(memory_space=pltpu.HBM)


def mm(a, b, ca=1, cb=0):
    return lax.dot_general(a, b, (((ca,), (cb,)), ((), ())), preferred_element_type=F32)


def slots_of(ids_row, peers):
    n = ids_row.shape[1]
    across = jnp.broadcast_to(ids_row, (n, n))
    down = across.T
    row = lax.broadcasted_iota(jnp.int32, (n, n), 0)
    col = lax.broadcasted_iota(jnp.int32, (n, n), 1)
    earlier = jnp.where((across == down) & (row < col), 1.0, 0.0).astype(F32)
    rank = jnp.sum(earlier, axis=0, keepdims=True).astype(jnp.int32)
    return rank * peers + ids_row


def placing_of(ids_row, peers):
    n = ids_row.shape[1]
    lines = lax.broadcasted_iota(jnp.int32, (CAP * peers, n), 0)
    return jnp.where(lines == slots_of(ids_row, peers), 1.0, 0.0).astype(BF16)


def lanes(q, count=1):
    return slice(q * LANE, (q + count) * LANE)


def start_all(pairs, sems, base=0):
    copies = [
        pltpu.make_async_copy(source, target, sems.at[base + i])
        for i, (source, target) in enumerate(pairs)
    ]
    for copy in copies:
        copy.start()
    return copies


def pack_kernel(
    peers, ids_ref, weight_ref, tok_hbm, cot_hbm, own_hbm,
    out_hbm, passed_hbm,
    tok, cot, own, out, scr, sems,
):
    copies = start_all([(tok_hbm, tok), (cot_hbm, cot), (own_hbm, own)], sems)
    n, width = tok.shape
    chunks = width // LANE
    placing = placing_of(ids_ref[...], peers)
    weight = jnp.broadcast_to(weight_ref[...], (n, n)).T[:, :1]
    copies[2].wait()
    sent = start_all([(own, passed_hbm)], sems, 5)
    for which in range(2):
        copies[which].wait()
        for c in range(0, chunks, 2):
            if which == 0:
                rows = tok[:, lanes(c, 2)]
            else:
                rows = (weight * cot[:, lanes(c, 2)].astype(F32)).astype(BF16)
            placed = mm(placing, rows)
            for s in range(CAP):
                for h in range(2):
                    scr[CAP * which + s, pl.ds(c + h, peers, stride=chunks), :] = placed[
                        s * peers : (s + 1) * peers, lanes(h)
                    ]
        for q in range(CAP * which, CAP * which + CAP):
            out[which, :, :, lanes(q % CAP)] = (
                scr[q].reshape(peers, chunks, LANE).astype(BF16)
            )
        copy = pltpu.make_async_copy(
            out.at[which], out_hbm.at[:, :, pl.ds(which * CAP * LANE, CAP * LANE)], sems.at[3 + which]
        )
        copy.start()
        sent.append(copy)
    for copy in sent:
        copy.wait()


def to_rows(got, scr):
    peers, chunks, _ = got.shape
    for s in range(CAP):
        scr[s] = got[:, :, lanes(s)].astype(F32).reshape(peers * chunks, LANE)
    for s in range(CAP):
        for c in range(chunks):
            yield slice(s * peers, (s + 1) * peers), c, scr[s, pl.ds(c, peers, stride=chunks), :]


def forward_kernel(
    place_ref, got_hbm, wg_hbm, wu_hbm, after_hbm,
    send_a_hbm, send_b_hbm, keep_a_hbm, keep_b_hbm, gate_hbm, up_hbm, cot_hbm,
    got, wg, wu, scr, rows, cot, own, other, gate, up, send, keep, sems,
):
    copies = start_all(
        [
            (got_hbm.at[:, :, pl.ds(0, CAP * LANE)], got.at[0]),
            (wg_hbm, wg),
            (wu_hbm, wu),
            (got_hbm.at[:, :, pl.ds(CAP * LANE, CAP * LANE)], got.at[1]),
        ],
        sems,
    )
    chunks = got.shape[2]
    z, core = place_ref[0], place_ref[1]
    first = core == 0
    copies[0].wait()
    for lines, c, value in to_rows(got.at[0], scr):
        rows[lines, lanes(c)] = value.astype(BF16)
    copies[1].wait()
    gate_value = mm(rows[...], wg[...])
    gate[...] = gate_value
    copies[2].wait()
    up_value = mm(rows[...], wu[...])
    up[...] = up_value
    hidden = (gate_value * jax.nn.sigmoid(gate_value) * up_value).astype(BF16)
    sent = start_all([(gate, gate_hbm), (up, up_hbm)], sems, 4)
    copies[3].wait()
    even = None
    for lines, c, value in to_rows(got.at[1], scr):
        cot[lines, lanes(c)] = value.astype(BF16)
        if c % 2 == 0:
            even = value
        else:
            own[lines, lanes(c // 2)] = jnp.where(first, even, value).astype(BF16)
            other[lines, lanes(c // 2)] = jnp.where(first, value, even).astype(BF16)
    sent += start_all([(cot, cot_hbm)], sems, 6)
    chips = chunks // 2
    half = chips // 2
    for i, (source, target, a_hbm, b_hbm, ahead) in enumerate(
        (
            (other, send, send_a_hbm, send_b_hbm, 2 * core - 1),
            (own, keep, keep_a_hbm, keep_b_hbm, 1 - 2 * core),
        )
    ):
        for b in range(0, chips, 2):
            value = mm(source[:, lanes(b, 2)], hidden, 0, 0).astype(BF16)
            target[b] = value[:LANE]
            target[b + 1] = value[LANE:]
        moves = []
        for at, step in enumerate(FOLD):
            chip = lax.rem(z + step * ahead + chips, chips)
            moves.append((target.at[chip], (a_hbm if at < half else b_hbm).at[at % half]))
        sent += start_all(moves, sems, 7 + i * chips)
    for copy in sent:
        copy.wait()


def backward_kernel(
    place_ref, gate_hbm, up_hbm, cot_hbm,
    first_hbm, rest_hbm, first_other_hbm, rest_other_hbm, wg_hbm, wu_hbm,
    part_hbm,
    gate, up, cot, down, wg, wu, scr, part, sems,
):
    z, core = place_ref[0], place_ref[1]
    near = first_hbm.shape[0]
    chips = near + rest_hbm.shape[0]
    gathered = []
    for i, step in enumerate(NEAR):
        ahead = step * (1 - 2 * core)
        mine, theirs = (first_hbm, first_other_hbm) if i < near else (rest_hbm, rest_other_hbm)
        at = i if i < near else i - near
        chip = lax.rem(z + ahead + chips, chips)
        gathered.append((mine.at[at], down.at[chip * 2 + core]))
        chip = lax.rem(z - ahead + chips, chips)
        gathered.append((theirs.at[at], down.at[chip * 2 + 1 - core]))
    copies = start_all([(cot_hbm, cot)], sems)
    arriving = start_all(gathered, sems, 7)
    copies += start_all(
        [(gate_hbm, gate), (up_hbm, up), (wg_hbm, wg), (wu_hbm, wu)], sems, 1
    )
    peers, chunks, _ = part.shape
    copies[0].wait()
    for copy in arriving:
        copy.wait()
    grad = mm(cot[...], down[...].reshape(wg.shape))
    copies[1].wait()
    copies[2].wait()
    v = gate[...]
    sig = jax.nn.sigmoid(v)
    gate_grad = (grad * up[...] * sig * (1.0 + v * (1.0 - sig))).astype(BF16)
    up_grad = (grad * (v * sig)).astype(BF16)
    copies[3].wait()
    copies[4].wait()
    for c in range(0, chunks, 2):
        at = lanes(c, 2)
        value = mm(gate_grad, wg[at, :], 1, 1) + mm(up_grad, wu[at, :], 1, 1)
        for s in range(CAP):
            for h in range(2):
                scr[s, pl.ds(c + h, peers, stride=chunks), :] = value[
                    s * peers : (s + 1) * peers, lanes(h)
                ]
    for s in range(CAP):
        part[:, :, lanes(s)] = scr[s].reshape(peers, chunks, LANE).astype(BF16)
    for copy in start_all([(part, part_hbm)], sems, 5):
        copy.wait()


def collect_kernel(peers, ids_ref, got_hbm, out_ref, mark_ref, got, scr, rows, sem):
    copy = pltpu.make_async_copy(got_hbm, got, sem)
    copy.start()
    placing = placing_of(ids_ref[...], peers)
    copy.wait()
    for lines, c, value in to_rows(got, scr):
        rows[lines, lanes(c)] = value.astype(BF16)
    out_ref[...] = mm(placing, rows[...], 0, 0).astype(BF16)
    mark_ref[...] = ids_ref[...]


def call(kernel, out_shape, in_specs, out_specs, scratch, limit, flops, moved, name):
    return pl.pallas_call(
        kernel,
        out_shape=out_shape,
        in_specs=in_specs,
        out_specs=out_specs,
        scratch_shapes=scratch,
        compiler_params=pltpu.CompilerParams(vmem_limit_bytes=limit << 20),
        cost_estimate=pl.CostEstimate(flops=flops, bytes_accessed=moved, transcendentals=0),
        name=name,
    )


def over_core(x):
    return lax.ppermute(x, "core", [(0, 1), (1, 0)])


def round_z(x, step):
    chips = lax.axis_size("z")
    pairs = [
        (2 * j + core, (j + step * (1 - 2 * core)) % chips * 2 + core)
        for j in range(chips)
        for core in range(2)
    ]
    return lax.ppermute(x, ("z", "core"), pairs)


def gather_features(own):
    m1, p1, m3, p3 = round_z(own, 1), round_z(own, -1), round_z(own, 3), round_z(own, -3)
    m2, m4 = jnp.split(round_z(jnp.concatenate([m1, m3]), 1), 2)
    p2 = round_z(p1, -1)
    first = jnp.stack([own, m1, p1, m3, p3])
    rest = jnp.stack([m2, m4, p2])
    return first, rest, over_core(first), over_core(rest)


def finish_kernel(total_ref, *refs):
    *arrived, _, out_ref = refs
    total = total_ref[...]
    for ref in arrived:
        total = total + ref[...].astype(F32)
    out_ref[...] = total.reshape(out_ref.shape)


def reduce_features(above, below, far_below, keep, swapped):
    outer, inner, under, total = [
        keep[i].astype(F32) + swapped[i].astype(F32) for i in range(keep.shape[0])
    ]
    far_above = round_z((outer + above[1].astype(F32)).astype(BF16), -3)
    near_above = round_z((inner + above[0].astype(F32)).astype(BF16), -1)
    near_below = round_z((under + below.astype(F32)).astype(BF16), 1)
    return total, near_above, far_above, near_below, far_below


def on_device(tokens, cotangent, expert_ids, route_weight, w_gate, w_up, w_down):
    n, width = tokens.shape
    peers = lax.axis_size("expert")
    ranks = lax.axis_size("z") * 2
    hidden = w_gate.shape[2]
    chunks = width // LANE
    slots = CAP * peers
    product = 2 * slots * width * hidden
    ids = expert_ids.reshape(1, n)
    weight = route_weight.reshape(1, n)
    wg = w_gate.reshape(width, hidden)
    wu = w_up.reshape(width, hidden)
    place = jnp.stack([lax.axis_index("z"), lax.axis_index("core")]).astype(jnp.int32)
    own = w_down.reshape(width // ranks, hidden)

    shape = jax.ShapeDtypeStruct
    packed, own = call(
        functools.partial(pack_kernel, peers),
        (shape((peers, chunks, 2 * CAP * LANE), BF16), shape(own.shape, BF16)),
        [VMEM, VMEM, HBM, HBM, HBM],
        (HBM, HBM),
        [
            pltpu.VMEM((n, width), BF16),
            pltpu.VMEM((n, width), BF16),
            pltpu.VMEM(own.shape, BF16),
            pltpu.VMEM((2, peers, chunks, CAP * LANE), BF16),
            pltpu.VMEM((2 * CAP, peers * chunks, LANE), F32),
            pltpu.SemaphoreType.DMA((6,)),
        ],
        58, 4 * slots * n * width, 4 << 20, "pack",
    )(ids, weight, tokens, cotangent, own)
    got = lax.all_to_all(packed, "expert", split_axis=0, concat_axis=0, tiled=True)
    gathered = gather_features(own)

    weights = pltpu.VMEM((width, hidden), BF16)
    features = pltpu.VMEM((chunks // 2, LANE, hidden), BF16)
    inner = pltpu.VMEM((slots, hidden), F32)
    quarter = shape((chunks // 4, LANE, hidden), BF16)
    send_a, send_b, keep_a, keep_b, gate, up, cot = call(
        forward_kernel,
        (
            quarter,
            quarter,
            quarter,
            quarter,
            shape((slots, hidden), F32),
            shape((slots, hidden), F32),
            shape((slots, width), BF16),
        ),
        [SMEM] + [HBM] * 4,
        (HBM,) * 7,
        [
            pltpu.VMEM((2, peers, chunks, CAP * LANE), BF16),
            weights,
            weights,
            pltpu.VMEM((CAP, peers * chunks, LANE), F32),
            pltpu.VMEM((slots, width), BF16),
            pltpu.VMEM((slots, width), BF16),
            pltpu.VMEM((slots, width // 2), BF16),
            pltpu.VMEM((slots, width // 2), BF16),
            inner,
            inner,
            features,
            features,
            pltpu.SemaphoreType.DMA((7 + chunks,)),
        ],
        62, 3 * product, 14 << 20, "forward",
    )(place, got, wg, wu, gathered[1])
    swapped_a = over_core(send_a)
    swapped_b = over_core(send_b)
    outward = (keep_a.astype(F32) + swapped_a.astype(F32)).astype(BF16)
    above = [round_z(outward[0], -1), round_z(outward[1], -1)]
    below = round_z(outward[2], 1)
    far_below = round_z(outward[3], 3)

    part = call(
        backward_kernel,
        shape((peers, chunks, CAP * LANE), BF16),
        [SMEM] + [HBM] * 9,
        HBM,
        [
            inner,
            inner,
            pltpu.VMEM((slots, width), BF16),
            pltpu.VMEM((chunks, LANE, hidden), BF16),
            weights,
            weights,
            pltpu.VMEM((CAP, peers * chunks, LANE), F32),
            pltpu.VMEM((peers, chunks, CAP * LANE), BF16),
            pltpu.SemaphoreType.DMA((7 + chunks,)),
        ],
        62, 3 * product, 14 << 20, "backward",
    )(place, gate, up, cot, *gathered, wg, wu)

    terms = reduce_features(above, below, far_below, keep_b, swapped_b)
    returned = lax.all_to_all(part, "expert", split_axis=0, concat_axis=0, tiled=True)

    token_grad, mark = call(
        functools.partial(collect_kernel, peers),
        (shape((n, width), BF16), shape((1, n), jnp.int32)),
        [VMEM, HBM],
        (VMEM, VMEM),
        [
            pltpu.VMEM((peers, chunks, CAP * LANE), BF16),
            pltpu.VMEM((CAP, peers * chunks, LANE), F32),
            pltpu.VMEM((slots, width), BF16),
            pltpu.SemaphoreType.DMA,
        ],
        16, 2 * slots * n * width, 2 << 20, "collect",
    )(ids, returned)
    down_grad = call(
        finish_kernel,
        shape((width // ranks, 1, hidden), F32),
        [VMEM] * (len(terms) + 1),
        VMEM,
        [],
        8, 5 * LANE * hidden, 2 << 20, "finish",
    )(*terms, mark)
    return (token_grad, down_grad)


def solution(mesh):
    ranks = mesh.shape["dp"]
    split = Mesh(
        mesh.devices.reshape(mesh.shape["expert"], ranks // 2, 2), ("expert", "z", "core")
    )
    tokens = P(("expert", "z", "core"), None)
    experts = P("expert", None, None)
    features = P(("z", "core"), "expert", None)
    return jax.shard_map(
        on_device,
        mesh=split,
        in_specs=(tokens, tokens, tokens, tokens, experts, experts, features),
        out_specs=(tokens, features),
        check_vma=False,
    )
```

```python
import functools

import jax
import jax.numpy as jnp
from jax import lax
from jax.experimental import pallas as pl
from jax.experimental.pallas import tpu as pltpu
from jax.sharding import Mesh, PartitionSpec as P

CAP = 3
LANE = 128
NEAR = (0, -1, 1, -3, 3, -2, -4, 2)
FOLD = (-2, -4, 2, 3, -3, -1, 1, 0)
BF16 = jnp.bfloat16
F32 = jnp.float32

VMEM = pl.BlockSpec(memory_space=pltpu.VMEM)
SMEM = pl.BlockSpec(memory_space=pltpu.SMEM)
HBM = pl.BlockSpec(memory_space=pltpu.HBM)


def mm(a, b, ca=1, cb=0):
    return lax.dot_general(a, b, (((ca,), (cb,)), ((), ())), preferred_element_type=F32)


def slots_of(ids_row, peers):
    n = ids_row.shape[1]
    across = jnp.broadcast_to(ids_row, (n, n))
    down = across.T
    row = lax.broadcasted_iota(jnp.int32, (n, n), 0)
    col = lax.broadcasted_iota(jnp.int32, (n, n), 1)
    earlier = jnp.where((across == down) & (row < col), 1.0, 0.0).astype(F32)
    rank = jnp.sum(earlier, axis=0, keepdims=True).astype(jnp.int32)
    return rank * peers + ids_row


def placing_of(ids_row, peers):
    n = ids_row.shape[1]
    lines = lax.broadcasted_iota(jnp.int32, (CAP * peers, n), 0)
    return jnp.where(lines == slots_of(ids_row, peers), 1.0, 0.0).astype(BF16)


def lanes(q, count=1):
    return slice(q * LANE, (q + count) * LANE)


def start_all(pairs, sems, base=0):
    copies = [
        pltpu.make_async_copy(source, target, sems.at[base + i])
        for i, (source, target) in enumerate(pairs)
    ]
    for copy in copies:
        copy.start()
    return copies


def pack_kernel(
    peers, ids_ref, weight_ref, tok_hbm, cot_hbm, own_hbm,
    out_hbm, passed_hbm,
    tok, cot, own, out, scr, sems,
):
    copies = start_all([(tok_hbm, tok), (cot_hbm, cot), (own_hbm, own)], sems)
    n, width = tok.shape
    chunks = width // LANE
    placing = placing_of(ids_ref[...], peers)
    weight = jnp.broadcast_to(weight_ref[...], (n, n)).T[:, :1]
    copies[2].wait()
    sent = start_all([(own, passed_hbm)], sems, 5)
    for which in range(2):
        copies[which].wait()
        for c in range(0, chunks, 2):
            if which == 0:
                rows = tok[:, lanes(c, 2)]
            else:
                rows = (weight * cot[:, lanes(c, 2)].astype(F32)).astype(BF16)
            placed = mm(placing, rows)
            for s in range(CAP):
                for h in range(2):
                    scr[CAP * which + s, pl.ds(c + h, peers, stride=chunks), :] = placed[
                        s * peers : (s + 1) * peers, lanes(h)
                    ]
        for q in range(CAP * which, CAP * which + CAP):
            out[which, :, :, lanes(q % CAP)] = (
                scr[q].reshape(peers, chunks, LANE).astype(BF16)
            )
        copy = pltpu.make_async_copy(
            out.at[which], out_hbm.at[:, :, pl.ds(which * CAP * LANE, CAP * LANE)], sems.at[3 + which]
        )
        copy.start()
        sent.append(copy)
    for copy in sent:
        copy.wait()


def to_rows(got, scr):
    peers, chunks, _ = got.shape
    for s in range(CAP):
        scr[s] = got[:, :, lanes(s)].astype(F32).reshape(peers * chunks, LANE)
    for s in range(CAP):
        for c in range(chunks):
            yield slice(s * peers, (s + 1) * peers), c, scr[s, pl.ds(c, peers, stride=chunks), :]


def forward_kernel(
    place_ref, got_hbm, wg_hbm, wu_hbm, after_hbm,
    send_a_hbm, send_b_hbm, keep_a_hbm, keep_b_hbm, gate_hbm, up_hbm, cot_hbm,
    got, wg, wu, scr, rows, cot, own, other, gate, up, send, keep, sems,
):
    copies = start_all(
        [
            (got_hbm.at[:, :, pl.ds(0, CAP * LANE)], got.at[0]),
            (wg_hbm, wg),
            (wu_hbm, wu),
            (got_hbm.at[:, :, pl.ds(CAP * LANE, CAP * LANE)], got.at[1]),
        ],
        sems,
    )
    chunks = got.shape[2]
    z, core = place_ref[0], place_ref[1]
    first = core == 0
    copies[0].wait()
    for lines, c, value in to_rows(got.at[0], scr):
        rows[lines, lanes(c)] = value.astype(BF16)
    copies[1].wait()
    gate_value = mm(rows[...], wg[...])
    gate[...] = gate_value
    copies[2].wait()
    up_value = mm(rows[...], wu[...])
    up[...] = up_value
    hidden = (gate_value * jax.nn.sigmoid(gate_value) * up_value).astype(BF16)
    sent = start_all([(gate, gate_hbm), (up, up_hbm)], sems, 4)
    copies[3].wait()
    even = None
    for lines, c, value in to_rows(got.at[1], scr):
        cot[lines, lanes(c)] = value.astype(BF16)
        if c % 2 == 0:
            even = value
        else:
            own[lines, lanes(c // 2)] = jnp.where(first, even, value).astype(BF16)
            other[lines, lanes(c // 2)] = jnp.where(first, value, even).astype(BF16)
    sent += start_all([(cot, cot_hbm)], sems, 6)
    chips = chunks // 2
    half = chips // 2
    for i, (source, target, a_hbm, b_hbm, ahead) in enumerate(
        (
            (other, send, send_a_hbm, send_b_hbm, 2 * core - 1),
            (own, keep, keep_a_hbm, keep_b_hbm, 1 - 2 * core),
        )
    ):
        for b in range(0, chips, 2):
            value = mm(source[:, lanes(b, 2)], hidden, 0, 0).astype(BF16)
            target[b] = value[:LANE]
            target[b + 1] = value[LANE:]
        moves = []
        for at, step in enumerate(FOLD):
            chip = lax.rem(z + step * ahead + chips, chips)
            moves.append((target.at[chip], (a_hbm if at < half else b_hbm).at[at % half]))
        sent += start_all(moves, sems, 7 + i * chips)
    for copy in sent:
        copy.wait()


def backward_kernel(
    place_ref, gate_hbm, up_hbm, cot_hbm,
    first_hbm, rest_hbm, first_other_hbm, rest_other_hbm, wg_hbm, wu_hbm,
    part_hbm,
    gate, up, cot, down, wg, wu, scr, part, sems,
):
    z, core = place_ref[0], place_ref[1]
    near = first_hbm.shape[0]
    chips = near + rest_hbm.shape[0]
    gathered = []
    for i, step in enumerate(NEAR):
        ahead = step * (1 - 2 * core)
        mine, theirs = (first_hbm, first_other_hbm) if i < near else (rest_hbm, rest_other_hbm)
        at = i if i < near else i - near
        chip = lax.rem(z + ahead + chips, chips)
        gathered.append((mine.at[at], down.at[chip * 2 + core]))
        chip = lax.rem(z - ahead + chips, chips)
        gathered.append((theirs.at[at], down.at[chip * 2 + 1 - core]))
    copies = start_all([(cot_hbm, cot)], sems)
    arriving = start_all(gathered, sems, 7)
    copies += start_all(
        [(gate_hbm, gate), (up_hbm, up), (wg_hbm, wg), (wu_hbm, wu)], sems, 1
    )
    peers, chunks, _ = part.shape
    copies[0].wait()
    for copy in arriving:
        copy.wait()
    grad = mm(cot[...], down[...].reshape(wg.shape))
    copies[1].wait()
    copies[2].wait()
    v = gate[...]
    sig = jax.nn.sigmoid(v)
    gate_grad = (grad * up[...] * sig * (1.0 + v * (1.0 - sig))).astype(BF16)
    up_grad = (grad * (v * sig)).astype(BF16)
    copies[3].wait()
    copies[4].wait()
    for c in range(0, chunks, 2):
        at = lanes(c, 2)
        value = mm(gate_grad, wg[at, :], 1, 1) + mm(up_grad, wu[at, :], 1, 1)
        for s in range(CAP):
            for h in range(2):
                scr[s, pl.ds(c + h, peers, stride=chunks), :] = value[
                    s * peers : (s + 1) * peers, lanes(h)
                ]
    for s in range(CAP):
        part[:, :, lanes(s)] = scr[s].reshape(peers, chunks, LANE).astype(BF16)
    for copy in start_all([(part, part_hbm)], sems, 5):
        copy.wait()


def collect_kernel(peers, ids_ref, got_hbm, out_ref, mark_ref, got, scr, rows, sem):
    copy = pltpu.make_async_copy(got_hbm, got, sem)
    copy.start()
    placing = placing_of(ids_ref[...], peers)
    copy.wait()
    for lines, c, value in to_rows(got, scr):
        rows[lines, lanes(c)] = value.astype(BF16)
    out_ref[...] = mm(placing, rows[...], 0, 0).astype(BF16)
    mark_ref[...] = ids_ref[...]


def call(kernel, out_shape, in_specs, out_specs, scratch, limit, flops, moved, name):
    return pl.pallas_call(
        kernel,
        out_shape=out_shape,
        in_specs=in_specs,
        out_specs=out_specs,
        scratch_shapes=scratch,
        compiler_params=pltpu.CompilerParams(vmem_limit_bytes=limit << 20),
        cost_estimate=pl.CostEstimate(flops=flops, bytes_accessed=moved, transcendentals=0),
        name=name,
    )


def over_core(x):
    return lax.ppermute(x, "core", [(0, 1), (1, 0)])


def round_z(x, step):
    chips = lax.axis_size("z")
    pairs = [
        (2 * j + core, (j + step * (1 - 2 * core)) % chips * 2 + core)
        for j in range(chips)
        for core in range(2)
    ]
    return lax.ppermute(x, ("z", "core"), pairs)


def gather_features(own):
    m1, p1, m3, p3 = round_z(own, 1), round_z(own, -1), round_z(own, 3), round_z(own, -3)
    m2, m4 = round_z(m1, 1), round_z(m3, 1)
    p2 = round_z(p1, -1)
    first = jnp.stack([own, m1, p1, m3, p3])
    rest = jnp.stack([m2, m4, p2])
    return first, rest, over_core(first), over_core(rest)


def finish_kernel(total_ref, *refs):
    *arrived, _, out_ref = refs
    total = total_ref[...]
    for ref in arrived:
        total = total + ref[...].astype(F32)
    out_ref[...] = total.reshape(out_ref.shape)


def reduce_features(above, below, far_below, keep, swapped):
    outer, inner, under, total = [
        keep[i].astype(F32) + swapped[i].astype(F32) for i in range(keep.shape[0])
    ]
    far_above = round_z((outer + above[1].astype(F32)).astype(BF16), -3)
    near_above = round_z((inner + above[0].astype(F32)).astype(BF16), -1)
    near_below = round_z((under + below.astype(F32)).astype(BF16), 1)
    return total, near_above, far_above, near_below, far_below


def on_device(tokens, cotangent, expert_ids, route_weight, w_gate, w_up, w_down):
    n, width = tokens.shape
    peers = lax.axis_size("expert")
    ranks = lax.axis_size("z") * 2
    hidden = w_gate.shape[2]
    chunks = width // LANE
    slots = CAP * peers
    product = 2 * slots * width * hidden
    ids = expert_ids.reshape(1, n)
    weight = route_weight.reshape(1, n)
    wg = w_gate.reshape(width, hidden)
    wu = w_up.reshape(width, hidden)
    place = jnp.stack([lax.axis_index("z"), lax.axis_index("core")]).astype(jnp.int32)
    own = w_down.reshape(width // ranks, hidden)

    shape = jax.ShapeDtypeStruct
    packed, own = call(
        functools.partial(pack_kernel, peers),
        (shape((peers, chunks, 2 * CAP * LANE), BF16), shape(own.shape, BF16)),
        [VMEM, VMEM, HBM, HBM, HBM],
        (HBM, HBM),
        [
            pltpu.VMEM((n, width), BF16),
            pltpu.VMEM((n, width), BF16),
            pltpu.VMEM(own.shape, BF16),
            pltpu.VMEM((2, peers, chunks, CAP * LANE), BF16),
            pltpu.VMEM((2 * CAP, peers * chunks, LANE), F32),
            pltpu.SemaphoreType.DMA((6,)),
        ],
        58, 4 * slots * n * width, 4 << 20, "pack",
    )(ids, weight, tokens, cotangent, own)
    got = lax.all_to_all(packed, "expert", split_axis=0, concat_axis=0, tiled=True)
    gathered = gather_features(own)

    weights = pltpu.VMEM((width, hidden), BF16)
    features = pltpu.VMEM((chunks // 2, LANE, hidden), BF16)
    inner = pltpu.VMEM((slots, hidden), F32)
    quarter = shape((chunks // 4, LANE, hidden), BF16)
    send_a, send_b, keep_a, keep_b, gate, up, cot = call(
        forward_kernel,
        (
            quarter,
            quarter,
            quarter,
            quarter,
            shape((slots, hidden), F32),
            shape((slots, hidden), F32),
            shape((slots, width), BF16),
        ),
        [SMEM] + [HBM] * 4,
        (HBM,) * 7,
        [
            pltpu.VMEM((2, peers, chunks, CAP * LANE), BF16),
            weights,
            weights,
            pltpu.VMEM((CAP, peers * chunks, LANE), F32),
            pltpu.VMEM((slots, width), BF16),
            pltpu.VMEM((slots, width), BF16),
            pltpu.VMEM((slots, width // 2), BF16),
            pltpu.VMEM((slots, width // 2), BF16),
            inner,
            inner,
            features,
            features,
            pltpu.SemaphoreType.DMA((7 + chunks,)),
        ],
        62, 3 * product, 14 << 20, "forward",
    )(place, got, wg, wu, gathered[1])
    swapped_a = over_core(send_a)
    swapped_b = over_core(send_b)
    outward = (keep_a.astype(F32) + swapped_a.astype(F32)).astype(BF16)
    above = [round_z(outward[0], -1), round_z(outward[1], -1)]
    below = round_z(outward[2], 1)
    far_below = round_z(outward[3], 3)

    part = call(
        backward_kernel,
        shape((peers, chunks, CAP * LANE), BF16),
        [SMEM] + [HBM] * 9,
        HBM,
        [
            inner,
            inner,
            pltpu.VMEM((slots, width), BF16),
            pltpu.VMEM((chunks, LANE, hidden), BF16),
            weights,
            weights,
            pltpu.VMEM((CAP, peers * chunks, LANE), F32),
            pltpu.VMEM((peers, chunks, CAP * LANE), BF16),
            pltpu.SemaphoreType.DMA((7 + chunks,)),
        ],
        62, 3 * product, 14 << 20, "backward",
    )(place, gate, up, cot, *gathered, wg, wu)

    terms = reduce_features(above, below, far_below, keep_b, swapped_b)
    returned = lax.all_to_all(part, "expert", split_axis=0, concat_axis=0, tiled=True)

    token_grad, mark = call(
        functools.partial(collect_kernel, peers),
        (shape((n, width), BF16), shape((1, n), jnp.int32)),
        [VMEM, HBM],
        (VMEM, VMEM),
        [
            pltpu.VMEM((peers, chunks, CAP * LANE), BF16),
            pltpu.VMEM((CAP, peers * chunks, LANE), F32),
            pltpu.VMEM((slots, width), BF16),
            pltpu.SemaphoreType.DMA,
        ],
        16, 2 * slots * n * width, 2 << 20, "collect",
    )(ids, returned)
    down_grad = call(
        finish_kernel,
        shape((width // ranks, 1, hidden), F32),
        [VMEM] * (len(terms) + 1),
        VMEM,
        [],
        8, 5 * LANE * hidden, 2 << 20, "finish",
    )(*terms, mark)
    return (token_grad, down_grad)


def solution(mesh):
    ranks = mesh.shape["dp"]
    split = Mesh(
        mesh.devices.reshape(mesh.shape["expert"], ranks // 2, 2), ("expert", "z", "core")
    )
    tokens = P(("expert", "z", "core"), None)
    experts = P("expert", None, None)
    features = P(("z", "core"), "expert", None)
    return jax.shard_map(
        on_device,
        mesh=split,
        in_specs=(tokens, tokens, tokens, tokens, experts, experts, features),
        out_specs=(tokens, features),
        check_vma=False,
    )
```
